32 devices in a mesh: dp: 4 (over x, core), cent: 8 (over z, y).
Axes of the slice: x: 2, y: 2, z: 4, core: 2. Of those that a mesh axis runs over, the one named last changes fastest.
Arguments:
- embeddings: bfloat16 [4096, 1536], P('dp'), may hold values from -1 to 1, as said below
- sharpness: float32 [4096], P('dp'), may hold values from 10 to 300
- centroids: bfloat16 [8192, 1536], P('cent'), may hold values from -1 to 1, as said below
Outputs:
- new_centroids: float32 [8192, 1536], P('cent', 'dp')
- residuals: bfloat16 [4096, 1536], P(('dp', 'cent'))
The draws below stay inside these ranges and needn't reach their ends.
Inputs may be any that keep to these rules, and one draw needn't show every extreme that they name: `embeddings`: each row has unit norm up to rounding. `centroids`: each row has unit norm up to rounding.
All inputs are finite; a program needn't handle non-finite values.
Results may differ from the reference program's by a relative error of at most 0.0034.
Values may be sent and summed in bfloat16 or wider, within the bound.
A program may use at most 64 MiB of HBM per device.

```python
import jax
import jax.numpy as jnp
from jax import lax

D = 1536
CENTROIDS = 8192
ROWS = 4096
N_DP = 4


def unit_rows(values):
    return values / jnp.sqrt(jnp.sum(values * values, axis=1, keepdims=True))


def cluster_count():
    return max(CENTROIDS // 256, 16)


def cluster_frame(key):
    groups = cluster_count()
    centers = unit_rows(jax.random.normal(jax.random.fold_in(key, 21), (groups, D), jnp.float32))
    drifts = unit_rows(jax.random.normal(jax.random.fold_in(key, 22), (groups, D), jnp.float32))
    return (centers, drifts)


def centroid_table(key):
    centers, drifts = cluster_frame(key)
    member = jax.random.randint(jax.random.fold_in(key, 23), (CENTROIDS,), 0, cluster_count())
    level = jax.random.uniform(jax.random.fold_in(key, 24), (CENTROIDS,), jnp.float32)
    spread = jnp.exp(jnp.log(0.25) + level * (jnp.log(1.2) - jnp.log(0.25)))
    noise = jax.random.normal(jax.random.fold_in(key, 11), (CENTROIDS, D), jnp.float32) * D ** (-0.5)
    return unit_rows(centers[member] + spread[:, None] * noise)


def draw_centroids(key, part):
    return centroid_table(key).astype(jnp.bfloat16)


def draw_embeddings(key, part):
    centers, drifts = cluster_frame(key)
    member = jax.random.randint(jax.random.fold_in(key, 25), (ROWS,), 0, cluster_count())
    noise = jax.random.normal(jax.random.fold_in(key, 12), (ROWS, D), jnp.float32) * D ** (-0.5)
    values = unit_rows(centers[member] + 0.5 * drifts[member] + 0.6 * noise)
    return values.astype(jnp.bfloat16)


def draw_sharpness(key, part):
    base = jax.random.uniform(jax.random.fold_in(key, 15), (ROWS,), jnp.float32)
    values = jnp.exp(jnp.log(10.0) + base * (jnp.log(100.0) - jnp.log(10.0)))
    return values


def setup_inputs(seed: int = 0) -> dict:
    splits = jax.random.split(jax.random.key(seed), 4)
    return {
        "embeddings": draw_embeddings(jax.random.fold_in(splits[3], 71), 0),
        "sharpness": draw_sharpness(jax.random.fold_in(splits[3], 71), 0),
        "centroids": draw_centroids(jax.random.fold_in(splits[3], 71), 0),
    }


def reference(embeddings, sharpness, centroids):
    rows_block = ROWS // N_DP
    emb_blocks = embeddings.reshape(N_DP, rows_block, D)
    sharp_blocks = sharpness.reshape(N_DP, rows_block)

    def step(carry, item):
        counts, update = carry
        block, sharp = item
        scores = jnp.dot(block, centroids.T, preferred_element_type=jnp.float32) * sharp[:, None]
        row_top = lax.optimization_barrier(jnp.max(scores, axis=1))
        weights = jnp.exp(scores - row_top[:, None])
        row_total = lax.optimization_barrier(jnp.sum(weights, axis=1))
        responsibility = (weights / row_total[:, None]).astype(jnp.bfloat16)
        mixture = jnp.dot(responsibility, centroids, preferred_element_type=jnp.float32)
        residual = (block.astype(jnp.float32) - mixture).astype(jnp.bfloat16)
        counts = counts + lax.optimization_barrier(jnp.sum(responsibility.astype(jnp.float32), axis=0))
        update = update + jnp.dot(responsibility.T, residual, preferred_element_type=jnp.float32)
        return ((counts, update), residual)
    init = (jnp.zeros((CENTROIDS,), jnp.float32), jnp.zeros((CENTROIDS, D), jnp.float32))
    (counts, update), residuals = lax.scan(step, init, (emb_blocks, sharp_blocks))
    moved = centroids.astype(jnp.float32) + update / (counts[:, None] + 1.0)
    new_centroids = moved * lax.rsqrt(lax.optimization_barrier(jnp.sum(moved * moved, axis=1)) + 1e-06)[:, None]
    return (new_centroids, residuals.reshape(ROWS, D))
```

```python
import functools

import jax
import jax.numpy as jnp
from jax import lax
from jax.experimental import pallas as pl
from jax.experimental.pallas import tpu as pltpu
from jax.sharding import PartitionSpec as P

MESH = pl.DeviceIdType.MESH
LANES = 128


def per_device_plain(embeddings, sharpness, centroids):
    scores = lax.dot_general(
        embeddings, centroids, (((1,), (1,)), ((), ())), preferred_element_type=jnp.float32
    )
    scores = scores * sharpness[:, None]
    row_top = lax.pmax(jnp.max(scores, axis=1), "cent")
    weights = jnp.exp(scores - row_top[:, None])
    row_total = lax.psum(jnp.sum(weights, axis=1), "cent")
    responsibility = (weights / row_total[:, None]).astype(jnp.bfloat16)
    partial_mixture = jnp.dot(responsibility, centroids, preferred_element_type=jnp.float32)
    share_rows = embeddings.shape[0] // lax.axis_size("cent")
    row_start = lax.axis_index("cent") * share_rows
    mixture_share = lax.psum_scatter(partial_mixture, "cent", scatter_dimension=0, tiled=True)
    own_rows = lax.dynamic_slice_in_dim(embeddings, row_start, share_rows, 0)
    own_residual = (own_rows.astype(jnp.float32) - mixture_share).astype(jnp.bfloat16)
    all_residual = lax.all_gather(own_residual, "cent", axis=0, tiled=True)
    count_part = jnp.sum(responsibility.astype(jnp.float32), axis=0)
    update = lax.dot_general(
        responsibility, all_residual, (((0,), (0,)), ((), ())), preferred_element_type=jnp.float32
    )
    width = centroids.shape[1] // lax.axis_size("dp")
    column_start = lax.axis_index("dp") * width
    centroid_cols = lax.dynamic_slice_in_dim(centroids, column_start, width, 1).astype(jnp.float32)
    counts = lax.psum(count_part, "dp")
    update_share = lax.psum_scatter(
        update.astype(jnp.bfloat16), "dp", scatter_dimension=1, tiled=True
    ).astype(jnp.float32)
    moved = centroid_cols + update_share / (counts[:, None] + 1.0)
    squares = lax.psum(jnp.sum(moved * moved, axis=1), "dp")
    new_centroids = moved * lax.rsqrt(squares + 1e-06)[:, None]
    return (new_centroids, own_residual)


def remote(src, dst, send_sem, recv_sem, target):
    return pltpu.make_async_remote_copy(
        src_ref=src, dst_ref=dst, send_sem=send_sem, recv_sem=recv_sem,
        device_id=target, device_id_type=MESH,
    )


def kernel(
    n_dp, n_cent, emb, sharp, cent, out_cent, out_res,
    weights, resp_t, resp, stats, y_out, y_in, y_own, z_out, z_in, z_own, res,
    upd_out, upd_in, upd_own, cnt, sq,
    st_s, st_r, y_s, y_r, z_s, z_r, gz_s, gz_r, gy_s, gy_r, u_s, u_r, c_s, c_r, q_s, q_r,
):
    f32, bf16 = jnp.float32, jnp.bfloat16
    rows, depth = emb.shape
    k = cent.shape[0]
    width = depth // n_dp
    nz = n_cent // 2
    share = rows // n_cent
    half = nz * share
    i = lax.axis_index("dp")
    j = lax.axis_index("cent")
    z, y = j // 2, j % 2
    partner = {"cent": z * 2 + (1 - y)}

    barrier = pltpu.get_barrier_semaphore()
    for d in range(1, n_cent):
        pl.semaphore_signal(
            barrier, inc=1, device_id={"cent": lax.rem(j + d, n_cent)}, device_id_type=MESH
        )
    for d in range(1, n_dp):
        pl.semaphore_signal(
            barrier, inc=1, device_id={"dp": lax.rem(i + d, n_dp)}, device_id_type=MESH
        )

    block = 2 * LANES if rows % (2 * LANES) == 0 else LANES

    def score_block(b, _):
        at = pl.ds(pl.multiple_of(b * block, block), block)
        s = lax.dot_general(
            cent[...], emb[at, :], (((1,), (1,)), ((), ())), preferred_element_type=f32
        ) * sharp[:, at]
        top = jnp.max(s, axis=0, keepdims=True)
        w = jnp.exp(s - top)
        weights[:, at] = w
        stats[j, 0:1, at] = top
        stats[j, 1:2, at] = jnp.sum(w, axis=0, keepdims=True)
        return 0

    lax.fori_loop(0, rows // block, score_block, 0)

    pl.semaphore_wait(barrier, n_cent - 1 + n_dp - 1)
    pending = []
    arrivals = []
    for d in range(1, n_cent):
        copy = remote(
            stats.at[j], stats.at[j], st_s.at[d - 1], st_r.at[d - 1],
            {"cent": lax.rem(j + d, n_cent)},
        )
        copy.start()
        pending.append(copy)
    for d in range(1, n_cent):
        src = lax.rem(j + n_cent - d, n_cent)
        remote(stats.at[src], stats.at[src], st_s.at[d - 1], st_r.at[d - 1], partner).wait_recv()

    tops = [stats[c, 0:1, :] for c in range(n_cent)]
    top = functools.reduce(jnp.maximum, tops)
    total = functools.reduce(
        jnp.add, [stats[c, 1:2, :] * jnp.exp(tops[c] - top) for c in range(n_cent)]
    )
    stats[n_cent, 0:1, :] = jnp.exp(stats[j, 0:1, :] - top) / total

    def resp_block(b, _):
        at = pl.ds(pl.multiple_of(b * share, share), share)
        r = weights[:, at] * stats[n_cent, 0:1, at]
        resp_t[:, at] = r.astype(bf16)
        to = pl.ds(pl.multiple_of((b // 2) * share, share), share)
        resp[b % 2, to, :] = r.T.astype(bf16)
        return 0

    lax.fori_loop(0, n_cent, resp_block, 0)

    def columns(s):
        owner = lax.rem(i + 1 + s, n_dp)
        return pl.ds(pl.multiple_of(owner * width, LANES), width)

    def mix(s):
        cols = cent[:, columns(s)]
        y_out[s] = jnp.dot(resp[1 - y], cols, preferred_element_type=f32).astype(bf16)
        copy = remote(y_out.at[s], y_in.at[s], y_s.at[s], y_r.at[s], partner)
        copy.start()
        pending.append(copy)
        y_own[s] = jnp.dot(resp[y], cols, preferred_element_type=f32).astype(bf16)

    def z_reduce(s):
        remote(y_out.at[s], y_in.at[s], y_s.at[s], y_r.at[s], partner).wait_recv()
        z_out[s] = (y_own[s].astype(f32) + y_in[s].astype(f32)).astype(bf16)
        for d in range(1, nz):
            tz = lax.rem(z + d, nz)
            src = z_out.at[s, pl.ds(pl.multiple_of(tz * share, share), share)]
            copy = remote(
                src, z_in.at[s, d - 1], z_s.at[s, d - 1], z_r.at[s, d - 1], {"cent": tz * 2 + y}
            )
            copy.start()
            pending.append(copy)

    def rows_of(block_index):
        return pl.ds(pl.multiple_of(block_index * share, share), share)

    def residual(s):
        acc = z_out[s, rows_of(z), :].astype(f32)
        for d in range(1, nz):
            remote(
                z_in.at[s, d - 1], z_in.at[s, d - 1], z_s.at[s, d - 1], z_r.at[s, d - 1], partner
            ).wait_recv()
            acc += z_in[s, d - 1].astype(f32)
        value = (emb[rows_of(j), columns(s)].astype(f32) - acc).astype(bf16)
        out_res[:, columns(s)] = value
        res[s, rows_of(j), :] = value
        here = res.at[s, rows_of(j)]
        for d in range(1, nz):
            copy = remote(
                here, here, gz_s.at[s, d - 1], gz_r.at[s, d - 1],
                {"cent": lax.rem(z + d, nz) * 2 + y},
            )
            copy.start()
            pending.append(copy)
        copy = remote(here, here, gy_s.at[s, 0], gy_r.at[s, 0], partner)
        copy.start()
        pending.append(copy)

    def forward(s):
        for d in range(1, nz):
            sz = lax.rem(z + nz - d, nz)
            here = res.at[s, rows_of(sz * 2 + y)]
            remote(here, here, gz_s.at[s, d - 1], gz_r.at[s, d - 1], partner).wait_recv()
            copy = remote(here, here, gy_s.at[s, d], gy_r.at[s, d], partner)
            copy.start()
            pending.append(copy)

    kb = min(k, 512)

    def update(s):
        for d in range(nz):
            sz = lax.rem(z + nz - d, nz)
            there = res.at[s, rows_of(sz * 2 + 1 - y)]
            remote(there, there, gy_s.at[s, d], gy_r.at[s, d], partner).wait_recv()

        def step(b, _):
            at = pl.ds(pl.multiple_of(b * kb, kb), kb)
            u = jnp.dot(resp_t[at, :], res[s], preferred_element_type=f32)
            if s < n_dp - 1:
                upd_out[s, at, :] = u.astype(bf16)
            else:
                upd_own[at, :] = u
            return 0

        lax.fori_loop(0, k // kb, step, 0)
        if s < n_dp - 1:
            copy = remote(
                upd_out.at[s], upd_in.at[s], u_s.at[s], u_r.at[s],
                {"dp": lax.rem(i + 1 + s, n_dp)},
            )
            copy.start()
            pending.append(copy)

    def share_rows_dp(buf, s_sem, r_sem):
        for d in range(1, n_dp):
            copy = remote(
                buf.at[0], buf.at[d], s_sem.at[d - 1], r_sem.at[d - 1],
                {"dp": lax.rem(i + d, n_dp)},
            )
            copy.start()
            pending.append(copy)

    def sum_rows_dp(buf, s_sem, r_sem):
        acc = buf[0]
        for d in range(1, n_dp):
            remote(
                buf.at[0], buf.at[d], s_sem.at[d - 1], r_sem.at[d - 1],
                {"dp": lax.rem(i + d, n_dp)},
            ).wait_recv()
            acc += buf[d]
        return jnp.broadcast_to(acc[0:1], (LANES, k)).T[:, 0:1]

    mix(0)
    for s in range(1, n_dp):
        mix(s)
    cnt[0] = lax.dot_general(
        jnp.ones((8, rows), bf16), resp_t[...], (((1,), (1,)), ((), ())),
        preferred_element_type=f32,
    )
    share_rows_dp(cnt, c_s, c_r)

    stages = (z_reduce, residual, forward, update)
    for t in range(n_dp + len(stages) - 1):
        for lag, stage in reversed(list(enumerate(stages))):
            if 0 <= t - lag < n_dp:
                stage(t - lag)

    inv = 1.0 / (sum_rows_dp(cnt, c_s, c_r) + 1.0)
    acc = upd_own[...]
    for s in range(n_dp - 1):
        remote(
            upd_out.at[s], upd_in.at[s], u_s.at[s], u_r.at[s], {"dp": lax.rem(i + 1 + s, n_dp)}
        ).wait_recv()
        acc += upd_in[s].astype(f32)
    own = pl.ds(pl.multiple_of(i * width, LANES), width)
    moved = cent[:, own].astype(f32) + acc * inv
    upd_own[...] = moved
    squares = jnp.sum(moved * moved, axis=1, keepdims=True)
    sq[0] = jnp.broadcast_to(squares, (k, LANES)).T[0:8]
    share_rows_dp(sq, q_s, q_r)
    norm = lax.rsqrt(sum_rows_dp(sq, q_s, q_r) + 1e-06)
    out_cent[...] = upd_own[...] * norm
    for copy in pending:
        copy.wait_send()


def per_device_fused(n_dp, n_cent, embeddings, sharpness, centroids):
    f32, bf16 = jnp.float32, jnp.bfloat16
    rows, depth = embeddings.shape
    k = centroids.shape[0]
    width = depth // n_dp
    nz = n_cent // 2
    share = rows // n_cent
    half = nz * share
    vmem = pl.BlockSpec(memory_space=pltpu.VMEM)
    dma = lambda *shape: pltpu.SemaphoreType.DMA(shape)
    pairs = lambda *shape: [dma(*shape), dma(*shape)]
    return pl.pallas_call(
        functools.partial(kernel, n_dp, n_cent),
        out_shape=(
            jax.ShapeDtypeStruct((k, width), f32),
            jax.ShapeDtypeStruct((share, depth), bf16),
        ),
        in_specs=[vmem] * 3,
        out_specs=(vmem, vmem),
        scratch_shapes=[
            pltpu.VMEM((k, rows), f32),
            pltpu.VMEM((k, rows), bf16),
            pltpu.VMEM((2, half, k), bf16),
            pltpu.VMEM((n_cent + 1, 2, rows), f32),
            pltpu.VMEM((n_dp, half, width), bf16),
            pltpu.VMEM((n_dp, half, width), bf16),
            pltpu.VMEM((n_dp, half, width), bf16),
            pltpu.VMEM((n_dp, half, width), bf16),
            pltpu.VMEM((n_dp, nz - 1, share, width), bf16),
            pltpu.VMEM((8, LANES), f32),
            pltpu.VMEM((n_dp, rows, width), bf16),
            pltpu.VMEM((n_dp - 1, k, width), bf16),
            pltpu.VMEM((n_dp - 1, k, width), bf16),
            pltpu.VMEM((k, width), f32),
            pltpu.VMEM((n_dp, 8, k), f32),
            pltpu.VMEM((n_dp, 8, k), f32),
        ]
        + pairs(n_cent - 1)
        + pairs(n_dp)
        + pairs(n_dp, nz - 1)
        + pairs(n_dp, nz - 1)
        + pairs(n_dp, nz)
        + pairs(n_dp - 1)
        + pairs(n_dp - 1)
        + pairs(n_dp - 1),
        compiler_params=pltpu.CompilerParams(
            collective_id=0, has_side_effects=True, vmem_limit_bytes=56 * 2**20
        ),
    )(embeddings, sharpness.reshape(1, rows), centroids)


def solution(mesh):
    n_dp, n_cent = mesh.shape["dp"], mesh.shape["cent"]

    def per_device(embeddings, sharpness, centroids):
        rows, depth = embeddings.shape
        fits = (
            n_dp > 1
            and n_cent > 2
            and n_cent % 2 == 0
            and depth % (n_dp * LANES) == 0
            and rows % (n_cent * LANES) == 0
            and centroids.shape[0] % 512 == 0
        )
        if fits:
            return per_device_fused(n_dp, n_cent, embeddings, sharpness, centroids)
        return per_device_plain(embeddings, sharpness, centroids)

    in_specs = (P("dp", None), P("dp"), P("cent", None))
    out_specs = (P("cent", "dp"), P(("dp", "cent"), None))
    return jax.shard_map(
        per_device, mesh=mesh, in_specs=in_specs, out_specs=out_specs, check_vma=False
    )
```

```python
import functools

import jax
import jax.numpy as jnp
from jax import lax
from jax.experimental import pallas as pl
from jax.experimental.pallas import tpu as pltpu
from jax.sharding import PartitionSpec as P

MESH = pl.DeviceIdType.MESH
LANES = 128


def per_device_plain(embeddings, sharpness, centroids):
    scores = lax.dot_general(
        embeddings, centroids, (((1,), (1,)), ((), ())), preferred_element_type=jnp.float32
    )
    scores = scores * sharpness[:, None]
    row_top = lax.pmax(jnp.max(scores, axis=1), "cent")
    weights = jnp.exp(scores - row_top[:, None])
    row_total = lax.psum(jnp.sum(weights, axis=1), "cent")
    responsibility = (weights / row_total[:, None]).astype(jnp.bfloat16)
    partial_mixture = jnp.dot(responsibility, centroids, preferred_element_type=jnp.float32)
    share_rows = embeddings.shape[0] // lax.axis_size("cent")
    row_start = lax.axis_index("cent") * share_rows
    mixture_share = lax.psum_scatter(partial_mixture, "cent", scatter_dimension=0, tiled=True)
    own_rows = lax.dynamic_slice_in_dim(embeddings, row_start, share_rows, 0)
    own_residual = (own_rows.astype(jnp.float32) - mixture_share).astype(jnp.bfloat16)
    all_residual = lax.all_gather(own_residual, "cent", axis=0, tiled=True)
    count_part = jnp.sum(responsibility.astype(jnp.float32), axis=0)
    update = lax.dot_general(
        responsibility, all_residual, (((0,), (0,)), ((), ())), preferred_element_type=jnp.float32
    )
    width = centroids.shape[1] // lax.axis_size("dp")
    column_start = lax.axis_index("dp") * width
    centroid_cols = lax.dynamic_slice_in_dim(centroids, column_start, width, 1).astype(jnp.float32)
    counts = lax.psum(count_part, "dp")
    update_share = lax.psum_scatter(
        update.astype(jnp.bfloat16), "dp", scatter_dimension=1, tiled=True
    ).astype(jnp.float32)
    moved = centroid_cols + update_share / (counts[:, None] + 1.0)
    squares = lax.psum(jnp.sum(moved * moved, axis=1), "dp")
    new_centroids = moved * lax.rsqrt(squares + 1e-06)[:, None]
    return (new_centroids, own_residual)


def remote(src, dst, send_sem, recv_sem, target):
    return pltpu.make_async_remote_copy(
        src_ref=src, dst_ref=dst, send_sem=send_sem, recv_sem=recv_sem,
        device_id=target, device_id_type=MESH,
    )


def kernel(
    n_dp, n_cent, emb, sharp, cent, out_cent, out_res,
    weights, resp_t, resp, stats, y_out, y_in, y_own, z_out, z_in, z_rel, z_acc, res,
    upd_out, upd_in, upd_own, cnt, sq,
    st_s, st_r, y_s, y_r, z_s, z_r, rl_s, rl_r, gz_s, gz_r, gf_s, gf_x, gy_s, gy_r,
    u_s, u_r, c_s, c_r, q_s, q_r,
):
    f32, bf16 = jnp.float32, jnp.bfloat16
    rows, depth = emb.shape
    k = cent.shape[0]
    width = depth // n_dp
    nz = n_cent // 2
    share = rows // n_cent
    half = nz * share
    groups = nz // 2
    pair = 2 * share
    relay = nz == 4
    i = lax.axis_index("dp")
    j = lax.axis_index("cent")
    z, y = j // 2, j % 2
    partner = {"cent": z * 2 + (1 - y)}
    inner = jnp.logical_and(z > 0, z < nz - 1)
    at_first, at_last = z == 0, z == nz - 1
    order = [nz - 1] + list(range(1, nz - 1)) if nz > 2 else [1]

    def rows_at(index):
        return pl.ds(pl.multiple_of(index * share, share), share)

    def place(zz, yy):
        return rows_at(yy * nz + zz)

    def zdev(zz):
        return {"cent": zz * 2 + y}

    barrier = pltpu.get_barrier_semaphore()
    for d in range(1, n_cent):
        pl.semaphore_signal(
            barrier, inc=1, device_id={"cent": lax.rem(j + d, n_cent)}, device_id_type=MESH
        )
    for d in range(1, n_dp):
        pl.semaphore_signal(
            barrier, inc=1, device_id={"dp": lax.rem(i + d, n_dp)}, device_id_type=MESH
        )

    pending = []

    def go(copy):
        copy.start()
        pending.append(copy.wait_send)

    def go_if(cond, copy):
        pl.when(cond)(copy.start)
        pending.append(lambda: pl.when(cond)(copy.wait_send))

    def score_group(g):
        def half_block(h, _):
            e = jnp.concatenate([emb[rows_at(4 * g + h), :], emb[rows_at(4 * g + 2 + h), :]], 0)
            sh = jnp.concatenate(
                [sharp[:, rows_at(4 * g + h)], sharp[:, rows_at(4 * g + 2 + h)]], 1
            )
            s = lax.dot_general(
                cent[...], e, (((1,), (1,)), ((), ())), preferred_element_type=f32
            ) * sh
            top = jnp.max(s, axis=0, keepdims=True)
            w = jnp.exp(s - top)
            weights[:, pl.ds(pl.multiple_of(h * half + g * pair, share), pair)] = w
            at = pl.ds(pl.multiple_of(h * pair, share), pair)
            stats[g, j, 0:1, at] = top
            stats[g, j, 1:2, at] = jnp.sum(w, axis=0, keepdims=True)
            return 0

        lax.fori_loop(0, 2, half_block, 0)

    def send_stats(g):
        here = stats.at[g, j]
        for d in range(1, n_cent):
            go(remote(
                here, here, st_s.at[g, d - 1], st_r.at[g, d - 1],
                {"cent": lax.rem(j + d, n_cent)},
            ))

    def respond(g):
        for d in range(1, n_cent):
            there = stats.at[g, lax.rem(j + n_cent - d, n_cent)]
            remote(there, there, st_s.at[g, d - 1], st_r.at[g, d - 1], partner).wait_recv()
        tops = [stats[g, c, 0:1, :] for c in range(n_cent)]
        top = functools.reduce(jnp.maximum, tops)
        total = functools.reduce(
            jnp.add, [stats[g, c, 1:2, :] * jnp.exp(tops[c] - top) for c in range(n_cent)]
        )
        stats[g, n_cent, 0:1, :] = jnp.exp(stats[g, j, 0:1, :] - top) / total

        def block(b, _):
            h, q = b // 2, b % 2
            at = place(2 * g + q, h)
            r = weights[:, at] * stats[g, n_cent, 0:1, rows_at(b)]
            resp_t[:, at] = r.astype(bf16)
            resp[h, rows_at(2 * g + q), :] = r.T.astype(bf16)
            return 0

        lax.fori_loop(0, 4, block, 0)

    def columns(s):
        owner = lax.rem(i + 1 + s, n_dp)
        return pl.ds(pl.multiple_of(owner * width, LANES), width)

    def y_copy(s, zz):
        at = rows_at(zz)
        return remote(y_out.at[s, at], y_in.at[s, at], y_s.at[s, zz], y_r.at[s, zz], partner)

    def mix_group(s, g):
        at = pl.ds(g * pair, pair)
        y_out[s, at, :] = jnp.dot(
            resp[1 - y, at, :], cent[:, columns(s)], preferred_element_type=f32
        ).astype(bf16)
        for q in range(2):
            go(y_copy(s, 2 * g + q))

    def mix_other(s):
        y_out[s] = jnp.dot(
            resp[1 - y], cent[:, columns(s)], preferred_element_type=f32
        ).astype(bf16)
        for d in order + [0]:
            go(y_copy(s, lax.rem(z + d, nz)))

    def mix_own(s):
        y_own[s] = jnp.dot(resp[y], cent[:, columns(s)], preferred_element_type=f32)

    def z_reduce(s):
        for d in order:
            tz = lax.rem(z + d, nz)
            at = rows_at(tz)
            y_copy(s, tz).wait_recv()
            value = y_own[s, at, :] + y_in[s, at, :].astype(f32)
            direct = remote(
                z_out.at[s, at], z_in.at[s, d - 1], z_s.at[s, d - 1], z_r.at[s, d - 1], zdev(tz)
            )
            z_out[s, at, :] = value.astype(bf16)
            if not relay:
                go(direct)
            elif d == 2:
                @pl.when(inner)
                def _():
                    remote(
                        z_rel.at[s], z_rel.at[s], rl_s.at[s], rl_r.at[s], partner
                    ).wait_recv()
                    z_out[s, at, :] = (value + z_rel[s].astype(f32)).astype(bf16)

                go(direct)
            else:
                far = at_last if d == 1 else at_first
                via = z - 1 if d == 1 else z + 1
                go_if(jnp.logical_not(far), direct)
                go_if(far, remote(
                    z_out.at[s, at], z_rel.at[s], rl_s.at[s], rl_r.at[s],
                    zdev(jnp.clip(via, 0, nz - 1)),
                ))

    def residual(s):
        at = rows_at(z)
        y_copy(s, z).wait_recv()
        z_acc[...] = y_own[s, at, :] + y_in[s, at, :].astype(f32)
        for d in order:
            def take(d=d):
                there = z_in.at[s, d - 1]
                remote(there, there, z_s.at[s, d - 1], z_r.at[s, d - 1], partner).wait_recv()
                z_acc[...] += z_in[s, d - 1].astype(f32)

            if relay and d != 2:
                pl.when(jnp.logical_not(at_first if d == 1 else at_last))(take)
            else:
                take()
        value = (emb[rows_at(j), columns(s)].astype(f32) - z_acc[...]).astype(bf16)
        out_res[:, columns(s)] = value
        res[s, place(z, y), :] = value
        here = res.at[s, place(z, y)]
        for d in ([2, 1, 3] if relay else order):
            copy = remote(
                here, here, gz_s.at[s, d - 1], gz_r.at[s, d - 1], zdev(lax.rem(z + d, nz))
            )
            if relay and d != 2:
                go_if(jnp.logical_not(at_last if d == 1 else at_first), copy)
            else:
                go(copy)
        go(remote(here, here, gy_s.at[s, 0], gy_r.at[s, 0], partner))

    def forward(s):
        for d in ([2, 1, 3] if relay else order):
            here = res.at[s, place(lax.rem(z + nz - d, nz), y)]
            remote(here, here, gz_s.at[s, d - 1], gz_r.at[s, d - 1], partner).wait_recv()
            if relay and d == 2:
                go_if(z == 2, remote(here, here, gf_s.at[s], gz_r.at[s, 2], zdev(3)))
                go_if(z == 1, remote(here, here, gf_x.at[s], gz_r.at[s, 0], zdev(0)))
            go(remote(here, here, gy_s.at[s, d], gy_r.at[s, d], partner))

    kb = min(k, 512)

    def update(s):
        for d in range(nz):
            there = res.at[s, place(lax.rem(z + nz - d, nz), 1 - y)]
            remote(there, there, gy_s.at[s, d], gy_r.at[s, d], partner).wait_recv()

        def step(b, _):
            at = pl.ds(pl.multiple_of(b * kb, kb), kb)
            u = jnp.dot(resp_t[at, :], res[s], preferred_element_type=f32)
            if s < n_dp - 1:
                upd_out[s, at, :] = u.astype(bf16)
            else:
                upd_own[at, :] = u
            return 0

        lax.fori_loop(0, k // kb, step, 0)
        if s < n_dp - 1:
            go(remote(
                upd_out.at[s], upd_in.at[s], u_s.at[s], u_r.at[s],
                {"dp": lax.rem(i + 1 + s, n_dp)},
            ))

    def share_rows_dp(buf, s_sem, r_sem):
        for d in range(1, n_dp):
            go(remote(
                buf.at[0], buf.at[d], s_sem.at[d - 1], r_sem.at[d - 1],
                {"dp": lax.rem(i + d, n_dp)},
            ))

    def sum_rows_dp(buf, s_sem, r_sem):
        acc = buf[0]
        for d in range(1, n_dp):
            remote(
                buf.at[0], buf.at[d], s_sem.at[d - 1], r_sem.at[d - 1],
                {"dp": lax.rem(i + d, n_dp)},
            ).wait_recv()
            acc += buf[d]
        return jnp.broadcast_to(acc[0:1], (LANES, k)).T[:, 0:1]

    score_group(0)
    pl.semaphore_wait(barrier, n_cent - 1 + n_dp - 1)
    send_stats(0)
    for g in range(1, groups):
        score_group(g)
        send_stats(g)
    for g in range(groups):
        respond(g)
        mix_group(0, g)
    mix_own(0)
    mix_other(1)
    mix_own(1)
    cnt[0] = lax.dot_general(
        jnp.ones((8, rows), bf16), resp_t[...], (((1,), (1,)), ((), ())),
        preferred_element_type=f32,
    )
    share_rows_dp(cnt, c_s, c_r)

    for t in range(n_dp + 3):
        if t < n_dp:
            z_reduce(t)
        if t + 2 < n_dp:
            mix_other(t + 2)
            mix_own(t + 2)
        if 0 <= t - 1 < n_dp:
            residual(t - 1)
        if 0 <= t - 2 < n_dp:
            forward(t - 2)
        if 0 <= t - 3 < n_dp:
            update(t - 3)

    inv = 1.0 / (sum_rows_dp(cnt, c_s, c_r) + 1.0)
    acc = upd_own[...]
    for s in range(n_dp - 1):
        remote(
            upd_out.at[s], upd_in.at[s], u_s.at[s], u_r.at[s], {"dp": lax.rem(i + 1 + s, n_dp)}
        ).wait_recv()
        acc += upd_in[s].astype(f32)
    own = pl.ds(pl.multiple_of(i * width, LANES), width)
    moved = cent[:, own].astype(f32) + acc * inv
    upd_own[...] = moved
    squares = jnp.sum(moved * moved, axis=1, keepdims=True)
    sq[0] = jnp.broadcast_to(squares, (k, LANES)).T[0:8]
    share_rows_dp(sq, q_s, q_r)
    norm = lax.rsqrt(sum_rows_dp(sq, q_s, q_r) + 1e-06)
    out_cent[...] = upd_own[...] * norm
    for wait in pending:
        wait()


def per_device_fused(n_dp, n_cent, embeddings, sharpness, centroids):
    f32, bf16 = jnp.float32, jnp.bfloat16
    rows, depth = embeddings.shape
    k = centroids.shape[0]
    width = depth // n_dp
    nz = n_cent // 2
    share = rows // n_cent
    half = nz * share
    vmem = pl.BlockSpec(memory_space=pltpu.VMEM)
    dma = lambda *shape: pltpu.SemaphoreType.DMA(shape)
    pairs = lambda *shape: [dma(*shape), dma(*shape)]
    return pl.pallas_call(
        functools.partial(kernel, n_dp, n_cent),
        out_shape=(
            jax.ShapeDtypeStruct((k, width), f32),
            jax.ShapeDtypeStruct((share, depth), bf16),
        ),
        in_specs=[vmem] * 3,
        out_specs=(vmem, vmem),
        scratch_shapes=[
            pltpu.VMEM((k, rows), f32),
            pltpu.VMEM((k, rows), bf16),
            pltpu.VMEM((2, half, k), bf16),
            pltpu.VMEM((nz // 2, n_cent + 1, 2, 4 * share), f32),
            pltpu.VMEM((n_dp, half, width), bf16),
            pltpu.VMEM((n_dp, half, width), bf16),
            pltpu.VMEM((n_dp, half, width), f32),
            pltpu.VMEM((n_dp, half, width), bf16),
            pltpu.VMEM((n_dp, nz - 1, share, width), bf16),
            pltpu.VMEM((n_dp, share, width), bf16),
            pltpu.VMEM((share, width), f32),
            pltpu.VMEM((n_dp, rows, width), bf16),
            pltpu.VMEM((n_dp - 1, k, width), bf16),
            pltpu.VMEM((n_dp - 1, k, width), bf16),
            pltpu.VMEM((k, width), f32),
            pltpu.VMEM((n_dp, 8, k), f32),
            pltpu.VMEM((n_dp, 8, k), f32),
        ]
        + pairs(nz // 2, n_cent - 1)
        + pairs(n_dp, nz)
        + pairs(n_dp, nz - 1)
        + pairs(n_dp)
        + pairs(n_dp, nz - 1)
        + pairs(n_dp)
        + pairs(n_dp, nz)
        + pairs(n_dp - 1)
        + pairs(n_dp - 1)
        + pairs(n_dp - 1),
        compiler_params=pltpu.CompilerParams(
            collective_id=0, has_side_effects=True, vmem_limit_bytes=56 * 2**20
        ),
    )(embeddings, sharpness.reshape(1, rows), centroids)


def solution(mesh):
    n_dp, n_cent = mesh.shape["dp"], mesh.shape["cent"]

    def per_device(embeddings, sharpness, centroids):
        rows, depth = embeddings.shape
        fits = (
            n_dp > 1
            and n_cent % 4 == 0
            and depth % (n_dp * LANES) == 0
            and rows % (n_cent * LANES) == 0
            and centroids.shape[0] % 512 == 0
        )
        if fits:
            return per_device_fused(n_dp, n_cent, embeddings, sharpness, centroids)
        return per_device_plain(embeddings, sharpness, centroids)

    in_specs = (P("dp", None), P("dp"), P("cent", None))
    out_specs = (P("cent", "dp"), P(("dp", "cent"), None))
    return jax.shard_map(
        per_device, mesh=mesh, in_specs=in_specs, out_specs=out_specs, check_vma=False
    )
```

```python
import functools

import jax
import jax.numpy as jnp
from jax import lax
from jax.experimental import pallas as pl
from jax.experimental.pallas import tpu as pltpu
from jax.sharding import PartitionSpec as P

MESH = pl.DeviceIdType.MESH
LANES = 128


def per_device_plain(embeddings, sharpness, centroids):
    scores = lax.dot_general(
        embeddings, centroids, (((1,), (1,)), ((), ())), preferred_element_type=jnp.float32
    )
    scores = scores * sharpness[:, None]
    row_top = lax.pmax(jnp.max(scores, axis=1), "cent")
    weights = jnp.exp(scores - row_top[:, None])
    row_total = lax.psum(jnp.sum(weights, axis=1), "cent")
    responsibility = (weights / row_total[:, None]).astype(jnp.bfloat16)
    partial_mixture = jnp.dot(responsibility, centroids, preferred_element_type=jnp.float32)
    share_rows = embeddings.shape[0] // lax.axis_size("cent")
    row_start = lax.axis_index("cent") * share_rows
    mixture_share = lax.psum_scatter(partial_mixture, "cent", scatter_dimension=0, tiled=True)
    own_rows = lax.dynamic_slice_in_dim(embeddings, row_start, share_rows, 0)
    own_residual = (own_rows.astype(jnp.float32) - mixture_share).astype(jnp.bfloat16)
    all_residual = lax.all_gather(own_residual, "cent", axis=0, tiled=True)
    count_part = jnp.sum(responsibility.astype(jnp.float32), axis=0)
    update = lax.dot_general(
        responsibility, all_residual, (((0,), (0,)), ((), ())), preferred_element_type=jnp.float32
    )
    width = centroids.shape[1] // lax.axis_size("dp")
    column_start = lax.axis_index("dp") * width
    centroid_cols = lax.dynamic_slice_in_dim(centroids, column_start, width, 1).astype(jnp.float32)
    counts = lax.psum(count_part, "dp")
    update_share = lax.psum_scatter(
        update.astype(jnp.bfloat16), "dp", scatter_dimension=1, tiled=True
    ).astype(jnp.float32)
    moved = centroid_cols + update_share / (counts[:, None] + 1.0)
    squares = lax.psum(jnp.sum(moved * moved, axis=1), "dp")
    new_centroids = moved * lax.rsqrt(squares + 1e-06)[:, None]
    return (new_centroids, own_residual)


def remote(src, dst, send_sem, recv_sem, target):
    return pltpu.make_async_remote_copy(
        src_ref=src, dst_ref=dst, send_sem=send_sem, recv_sem=recv_sem,
        device_id=target, device_id_type=MESH,
    )


def kernel(
    n_dp, n_cent, emb_in, sharp, cent_in, out_cent, out_res, emb, cent,
    weights, resp_t, resp, stats, y_out, y_in, y_own, z_out, z_in, z_rel, z_acc, res,
    upd_out, upd_in, upd_own, cnt, sq,
    st_s, st_r, y_s, y_r, z_s, z_r, rl_s, rl_r, gz_s, gz_r, gf_s, gf_x, gy_s, gy_r,
    hz_s, hz_r, hf_s, u_s, u_r, c_s, c_r, q_s, q_r, e_s,
):
    f32, bf16 = jnp.float32, jnp.bfloat16
    rows, depth = emb.shape
    k = cent.shape[0]
    width = depth // n_dp
    nz = n_cent // 2
    share = rows // n_cent
    half = nz * share
    pair = 2 * share
    early = n_dp - 2
    relay = nz == 4
    i = lax.axis_index("dp")
    j = lax.axis_index("cent")
    z, y = j // 2, j % 2
    partner = {"cent": z * 2 + (1 - y)}
    inner = jnp.logical_and(z > 0, z < nz - 1)
    at_first, at_last = z == 0, z == nz - 1
    order = [nz - 1] + list(range(1, nz - 1)) if nz > 2 else [1]

    def rows_at(index):
        return pl.ds(pl.multiple_of(index * share, share), share)

    def place(zz, yy):
        return rows_at(zz * 2 + yy)

    def zdev(zz):
        return {"cent": zz * 2 + y}

    barrier = pltpu.get_barrier_semaphore()
    for d in range(1, n_cent):
        pl.semaphore_signal(
            barrier, inc=1, device_id={"cent": lax.rem(j + d, n_cent)}, device_id_type=MESH
        )
    for d in range(1, n_dp):
        pl.semaphore_signal(
            barrier, inc=1, device_id={"dp": lax.rem(i + d, n_dp)}, device_id_type=MESH
        )

    pending = []

    def go(copy):
        copy.start()
        pending.append(copy.wait_send)

    def go_if(cond, copy):
        pl.when(cond)(copy.start)
        pending.append(lambda: pl.when(cond)(copy.wait_send))

    def pair_rows(g):
        return pl.ds(g * pair, pair)

    loads = [pltpu.make_async_copy(cent_in, cent, e_s.at[nz])] + [
        pltpu.make_async_copy(emb_in.at[pair_rows(g)], emb.at[pair_rows(g)], e_s.at[g])
        for g in range(nz)
    ]
    for load in loads:
        load.start()
    loads[0].wait()

    def score_group(g):
        loads[1 + g].wait()
        at = pair_rows(g)
        s = lax.dot_general(
            cent[...], emb[at, :], (((1,), (1,)), ((), ())), preferred_element_type=f32
        ) * sharp[:, at]
        top = jnp.max(s, axis=0, keepdims=True)
        w = jnp.exp(s - top)
        weights[:, at] = w
        stats[g, j, 0:1, :] = top
        stats[g, j, 1:2, :] = jnp.sum(w, axis=0, keepdims=True)

    def send_stats(g):
        here = stats.at[g, j]
        for d in range(1, n_cent):
            go(remote(
                here, here, st_s.at[g, d - 1], st_r.at[g, d - 1],
                {"cent": lax.rem(j + d, n_cent)},
            ))

    def respond(g):
        for d in range(1, n_cent):
            there = stats.at[g, lax.rem(j + n_cent - d, n_cent)]
            remote(there, there, st_s.at[g, d - 1], st_r.at[g, d - 1], partner).wait_recv()
        tops = [stats[g, c, 0:1, :] for c in range(n_cent)]
        top = functools.reduce(jnp.maximum, tops)
        total = functools.reduce(
            jnp.add, [stats[g, c, 1:2, :] * jnp.exp(tops[c] - top) for c in range(n_cent)]
        )
        scale = jnp.exp(stats[g, j, 0:1, :] - top) / total
        r = weights[:, pair_rows(g)] * scale
        resp_t[:, pair_rows(g)] = r.astype(bf16)
        for h in range(2):
            resp[h, rows_at(g), :] = r[:, h * share:(h + 1) * share].T.astype(bf16)

    def columns(s):
        owner = lax.rem(i + 1 + s, n_dp)
        return pl.ds(pl.multiple_of(owner * width, LANES), width)

    def y_copy(s, zz):
        at = rows_at(zz)
        return remote(y_out.at[s, at], y_in.at[s, at], y_s.at[s, zz], y_r.at[s, zz], partner)

    def mix_group(s, g):
        at = rows_at(g)
        y_out[s, at, :] = jnp.dot(
            resp[1 - y, at, :], cent[:, columns(s)], preferred_element_type=f32
        ).astype(bf16)
        go(y_copy(s, g))

    def mix_other(s):
        y_out[s] = jnp.dot(
            resp[1 - y], cent[:, columns(s)], preferred_element_type=f32
        ).astype(bf16)
        for d in order + [0]:
            go(y_copy(s, lax.rem(z + d, nz)))

    def mix_own(s):
        y_own[s] = jnp.dot(resp[y], cent[:, columns(s)], preferred_element_type=f32)

    def z_reduce(s):
        for d in order:
            tz = lax.rem(z + d, nz)
            at = rows_at(tz)
            y_copy(s, tz).wait_recv()
            value = y_own[s, at, :] + y_in[s, at, :].astype(f32)
            direct = remote(
                z_out.at[s, at], z_in.at[s, d - 1], z_s.at[s, d - 1], z_r.at[s, d - 1], zdev(tz)
            )
            z_out[s, at, :] = value.astype(bf16)
            if not relay:
                go(direct)
            elif d == 2:
                @pl.when(inner)
                def _():
                    remote(
                        z_rel.at[s], z_rel.at[s], rl_s.at[s], rl_r.at[s], partner
                    ).wait_recv()
                    z_out[s, at, :] = (value + z_rel[s].astype(f32)).astype(bf16)

                go(direct)
            else:
                far = at_last if d == 1 else at_first
                via = z - 1 if d == 1 else z + 1
                go_if(jnp.logical_not(far), direct)
                go_if(far, remote(
                    z_out.at[s, at], z_rel.at[s], rl_s.at[s], rl_r.at[s],
                    zdev(jnp.clip(via, 0, nz - 1)),
                ))

    def residual(s):
        at = rows_at(z)
        y_copy(s, z).wait_recv()
        z_acc[...] = y_own[s, at, :] + y_in[s, at, :].astype(f32)
        for d in order:
            def take(d=d):
                there = z_in.at[s, d - 1]
                remote(there, there, z_s.at[s, d - 1], z_r.at[s, d - 1], partner).wait_recv()
                z_acc[...] += z_in[s, d - 1].astype(f32)

            if relay and d != 2:
                pl.when(jnp.logical_not(at_first if d == 1 else at_last))(take)
            else:
                take()
        value = (emb[rows_at(j), columns(s)].astype(f32) - z_acc[...]).astype(bf16)
        out_res[:, columns(s)] = value
        res[s, place(z, y), :] = value
        here = res.at[s, place(z, y)]
        if s == early:
            go(remote(here, here, gy_s.at[s, 0], gy_r.at[s, 0], partner))
        spread(here, lambda d: (gz_s.at[s, d - 1], gz_r.at[s, d - 1]))
        if s != early:
            go(remote(here, here, gy_s.at[s, 0], gy_r.at[s, 0], partner))

    z_order = [2, 1, 3] if relay else order

    def spread(here, sems):
        for d in z_order:
            copy = remote(here, here, *sems(d), zdev(lax.rem(z + d, nz)))
            if relay and d != 2:
                go_if(jnp.logical_not(at_last if d == 1 else at_first), copy)
            else:
                go(copy)

    def arrive(s, d, yy, sems, onward):
        here = res.at[s, place(lax.rem(z + nz - d, nz), yy)]
        remote(here, here, *sems(d), partner).wait_recv()
        if relay and d == 2:
            go_if(z == 2, remote(here, here, onward(0), sems(3)[1], zdev(3)))
            go_if(z == 1, remote(here, here, onward(1), sems(1)[1], zdev(0)))
        return here

    def forward(s):
        own = lambda d: (gz_s.at[s, d - 1], gz_r.at[s, d - 1])
        other = lambda d: (hz_s.at[d - 1], hz_r.at[d - 1])
        if s == early:
            here = res.at[s, place(z, 1 - y)]
            remote(here, here, gy_s.at[s, 0], gy_r.at[s, 0], partner).wait_recv()
            spread(here, other)
        for d in z_order:
            here = arrive(s, d, y, own, lambda way: (gf_s if way == 0 else gf_x).at[s])
            if s == early:
                arrive(s, d, 1 - y, other, lambda way: hf_s.at[way])
            else:
                go(remote(here, here, gy_s.at[s, d], gy_r.at[s, d], partner))

    kb = min(k, 512)

    def update(s):
        for d in range(nz if s != early else 0):
            there = res.at[s, place(lax.rem(z + nz - d, nz), 1 - y)]
            remote(there, there, gy_s.at[s, d], gy_r.at[s, d], partner).wait_recv()

        def step(b, _):
            at = pl.ds(pl.multiple_of(b * kb, kb), kb)
            u = jnp.dot(resp_t[at, :], res[s], preferred_element_type=f32)
            if s < n_dp - 1:
                upd_out[s, at, :] = u.astype(bf16)
            else:
                upd_own[at, :] = u
            return 0

        lax.fori_loop(0, k // kb, step, 0)
        if s < n_dp - 1:
            go(remote(
                upd_out.at[s], upd_in.at[s], u_s.at[s], u_r.at[s],
                {"dp": lax.rem(i + 1 + s, n_dp)},
            ))

    def share_rows_dp(buf, s_sem, r_sem):
        for d in range(1, n_dp):
            go(remote(
                buf.at[0], buf.at[d], s_sem.at[d - 1], r_sem.at[d - 1],
                {"dp": lax.rem(i + d, n_dp)},
            ))

    def sum_rows_dp(buf, s_sem, r_sem):
        acc = buf[0]
        for d in range(1, n_dp):
            remote(
                buf.at[0], buf.at[d], s_sem.at[d - 1], r_sem.at[d - 1],
                {"dp": lax.rem(i + d, n_dp)},
            ).wait_recv()
            acc += buf[d]
        return jnp.broadcast_to(acc[0:1], (LANES, k)).T[:, 0:1]

    score_group(0)
    pl.semaphore_wait(barrier, n_cent - 1 + n_dp - 1)
    send_stats(0)
    lead = min(3, nz)
    for g in range(1, lead):
        score_group(g)
        send_stats(g)
    for g in range(nz):
        respond(g)
        mix_group(0, g)
        if g + lead < nz:
            score_group(g + lead)
            send_stats(g + lead)
    mix_own(0)
    mix_other(1)
    mix_own(1)
    cnt[0] = lax.dot_general(
        jnp.ones((8, rows), bf16), resp_t[...], (((1,), (1,)), ((), ())),
        preferred_element_type=f32,
    )
    share_rows_dp(cnt, c_s, c_r)

    for t in range(n_dp + 3):
        if t < n_dp:
            z_reduce(t)
        if t + 2 < n_dp:
            mix_other(t + 2)
            mix_own(t + 2)
        if 0 <= t - 1 < n_dp:
            residual(t - 1)
        if 0 <= t - 2 < n_dp:
            forward(t - 2)
        if 0 <= t - 3 < n_dp:
            update(t - 3)

    inv = 1.0 / (sum_rows_dp(cnt, c_s, c_r) + 1.0)
    acc = upd_own[...]
    for s in range(n_dp - 1):
        remote(
            upd_out.at[s], upd_in.at[s], u_s.at[s], u_r.at[s], {"dp": lax.rem(i + 1 + s, n_dp)}
        ).wait_recv()
        acc += upd_in[s].astype(f32)
    own = pl.ds(pl.multiple_of(i * width, LANES), width)
    moved = cent[:, own].astype(f32) + acc * inv
    upd_own[...] = moved
    squares = jnp.sum(moved * moved, axis=1, keepdims=True)
    sq[0] = jnp.broadcast_to(squares, (k, LANES)).T[0:8]
    share_rows_dp(sq, q_s, q_r)
    norm = lax.rsqrt(sum_rows_dp(sq, q_s, q_r) + 1e-06)
    out_cent[...] = upd_own[...] * norm
    for wait in pending:
        wait()


def hand_over(pieces, a, b, out_a, out_b, sem):
    size = a.shape[0] // pieces
    copies = [pltpu.make_async_copy(b, out_b, sem.at[pieces])]
    for p in range(pieces):
        at = pl.ds(p * size, size)
        copies.append(pltpu.make_async_copy(a.at[at], out_a.at[at], sem.at[p]))
    for copy in copies:
        copy.start()
    for copy in copies:
        copy.wait()


def per_device_fused(n_dp, n_cent, embeddings, sharpness, centroids):
    f32, bf16 = jnp.float32, jnp.bfloat16
    rows, depth = embeddings.shape
    k = centroids.shape[0]
    width = depth // n_dp
    nz = n_cent // 2
    share = rows // n_cent
    half = nz * share
    vmem = pl.BlockSpec(memory_space=pltpu.VMEM)
    hbm = pl.BlockSpec(memory_space=pl.ANY)
    dma = lambda *shape: pltpu.SemaphoreType.DMA(shape)
    pairs = lambda *shape: [dma(*shape), dma(*shape)]
    moved, own = pl.pallas_call(
        functools.partial(kernel, n_dp, n_cent),
        out_shape=(
            jax.ShapeDtypeStruct((k, width), f32),
            jax.ShapeDtypeStruct((share, depth), bf16),
        ),
        in_specs=[hbm, vmem, hbm],
        out_specs=(vmem, vmem),
        scratch_shapes=[
            pltpu.VMEM((rows, depth), bf16),
            pltpu.VMEM((k, depth), bf16),
            pltpu.VMEM((k, rows), f32),
            pltpu.VMEM((k, rows), bf16),
            pltpu.VMEM((2, half, k), bf16),
            pltpu.VMEM((nz, n_cent, 2, 2 * share), f32),
            pltpu.VMEM((n_dp, half, width), bf16),
            pltpu.VMEM((n_dp, half, width), bf16),
            pltpu.VMEM((n_dp, half, width), f32),
            pltpu.VMEM((n_dp, half, width), bf16),
            pltpu.VMEM((n_dp, nz - 1, share, width), bf16),
            pltpu.VMEM((n_dp, share, width), bf16),
            pltpu.VMEM((share, width), f32),
            pltpu.VMEM((n_dp, rows, width), bf16),
            pltpu.VMEM((n_dp - 1, k, width), bf16),
            pltpu.VMEM((n_dp - 1, k, width), bf16),
            pltpu.VMEM((k, width), f32),
            pltpu.VMEM((n_dp, 8, k), f32),
            pltpu.VMEM((n_dp, 8, k), f32),
        ]
        + pairs(nz, n_cent - 1)
        + pairs(n_dp, nz)
        + pairs(n_dp, nz - 1)
        + pairs(n_dp)
        + pairs(n_dp, nz - 1)
        + pairs(n_dp)
        + pairs(n_dp, nz)
        + pairs(nz - 1)
        + [dma(2)]
        + pairs(n_dp - 1)
        + pairs(n_dp - 1)
        + pairs(n_dp - 1)
        + [dma(nz + 1)],
        compiler_params=pltpu.CompilerParams(
            collective_id=0, has_side_effects=True, vmem_limit_bytes=56 * 2**20
        ),
    )(embeddings, sharpness.reshape(1, rows), centroids)
    pieces = 4
    return pl.pallas_call(
        functools.partial(hand_over, pieces),
        out_shape=(
            jax.ShapeDtypeStruct((k, width), f32),
            jax.ShapeDtypeStruct((share, depth), bf16),
        ),
        in_specs=[hbm, hbm],
        out_specs=(hbm, hbm),
        scratch_shapes=[dma(pieces + 1)],
    )(moved, own)


def solution(mesh):
    n_dp, n_cent = mesh.shape["dp"], mesh.shape["cent"]

    def per_device(embeddings, sharpness, centroids):
        rows, depth = embeddings.shape
        fits = (
            n_dp > 1
            and n_cent % 4 == 0
            and depth % (n_dp * LANES) == 0
            and rows % (n_cent * LANES) == 0
            and centroids.shape[0] % 512 == 0
        )
        if fits:
            return per_device_fused(n_dp, n_cent, embeddings, sharpness, centroids)
        return per_device_plain(embeddings, sharpness, centroids)

    in_specs = (P("dp", None), P("dp"), P("cent", None))
    out_specs = (P("cent", "dp"), P(("dp", "cent"), None))
    return jax.shard_map(
        per_device, mesh=mesh, in_specs=in_specs, out_specs=out_specs, check_vma=False
    )
```

```python
import functools

import jax
import jax.numpy as jnp
from jax import lax
from jax.experimental import pallas as pl
from jax.experimental.pallas import tpu as pltpu
from jax.sharding import PartitionSpec as P

MESH = pl.DeviceIdType.MESH
LANES = 128


def per_device_plain(embeddings, sharpness, centroids):
    scores = lax.dot_general(
        embeddings, centroids, (((1,), (1,)), ((), ())), preferred_element_type=jnp.float32
    )
    scores = scores * sharpness[:, None]
    row_top = lax.pmax(jnp.max(scores, axis=1), "cent")
    weights = jnp.exp(scores - row_top[:, None])
    row_total = lax.psum(jnp.sum(weights, axis=1), "cent")
    responsibility = (weights / row_total[:, None]).astype(jnp.bfloat16)
    partial_mixture = jnp.dot(responsibility, centroids, preferred_element_type=jnp.float32)
    share_rows = embeddings.shape[0] // lax.axis_size("cent")
    row_start = lax.axis_index("cent") * share_rows
    mixture_share = lax.psum_scatter(partial_mixture, "cent", scatter_dimension=0, tiled=True)
    own_rows = lax.dynamic_slice_in_dim(embeddings, row_start, share_rows, 0)
    own_residual = (own_rows.astype(jnp.float32) - mixture_share).astype(jnp.bfloat16)
    all_residual = lax.all_gather(own_residual, "cent", axis=0, tiled=True)
    count_part = jnp.sum(responsibility.astype(jnp.float32), axis=0)
    update = lax.dot_general(
        responsibility, all_residual, (((0,), (0,)), ((), ())), preferred_element_type=jnp.float32
    )
    width = centroids.shape[1] // lax.axis_size("dp")
    column_start = lax.axis_index("dp") * width
    centroid_cols = lax.dynamic_slice_in_dim(centroids, column_start, width, 1).astype(jnp.float32)
    counts = lax.psum(count_part, "dp")
    update_share = lax.psum_scatter(
        update.astype(jnp.bfloat16), "dp", scatter_dimension=1, tiled=True
    ).astype(jnp.float32)
    moved = centroid_cols + update_share / (counts[:, None] + 1.0)
    squares = lax.psum(jnp.sum(moved * moved, axis=1), "dp")
    new_centroids = moved * lax.rsqrt(squares + 1e-06)[:, None]
    return (new_centroids, own_residual)


def remote(src, dst, send_sem, recv_sem, target):
    return pltpu.make_async_remote_copy(
        src_ref=src, dst_ref=dst, send_sem=send_sem, recv_sem=recv_sem,
        device_id=target, device_id_type=MESH,
    )


def kernel(
    n_dp, n_cent, emb_in, sharp, cent_in, out_cent, out_res, emb, cent,
    weights, resp_t, resp, stats, y_out, y_in, y_own, z_out, z_in, z_rel, z_acc, res,
    upd_out, upd_in, upd_own, cnt, sq,
    st_s, st_r, y_s, y_r, z_s, z_r, rl_s, rl_r, gz_s, gz_r, gf_s, gf_x, gy_s, gy_r,
    u_s, u_r, c_s, c_r, q_s, q_r, e_s,
):
    f32, bf16 = jnp.float32, jnp.bfloat16
    rows, depth = emb.shape
    k = cent.shape[0]
    width = depth // n_dp
    nz = n_cent // 2
    share = rows // n_cent
    half = nz * share
    pair = 2 * share
    relay = nz == 4
    i = lax.axis_index("dp")
    j = lax.axis_index("cent")
    z, y = j // 2, j % 2
    partner = {"cent": z * 2 + (1 - y)}
    inner = jnp.logical_and(z > 0, z < nz - 1)
    at_first, at_last = z == 0, z == nz - 1
    order = [nz - 1] + list(range(1, nz - 1)) if nz > 2 else [1]

    def rows_at(index):
        return pl.ds(pl.multiple_of(index * share, share), share)

    def place(zz, yy):
        return rows_at(zz * 2 + yy)

    def zdev(zz):
        return {"cent": zz * 2 + y}

    barrier = pltpu.get_barrier_semaphore()
    for d in range(1, n_cent):
        pl.semaphore_signal(
            barrier, inc=1, device_id={"cent": lax.rem(j + d, n_cent)}, device_id_type=MESH
        )
    for d in range(1, n_dp):
        pl.semaphore_signal(
            barrier, inc=1, device_id={"dp": lax.rem(i + d, n_dp)}, device_id_type=MESH
        )

    pending = []

    def go(copy):
        copy.start()
        pending.append(copy.wait_send)

    def go_if(cond, copy):
        pl.when(cond)(copy.start)
        pending.append(lambda: pl.when(cond)(copy.wait_send))

    def pair_rows(g):
        return pl.ds(g * pair, pair)

    loads = [pltpu.make_async_copy(cent_in, cent, e_s.at[nz])] + [
        pltpu.make_async_copy(emb_in.at[pair_rows(g)], emb.at[pair_rows(g)], e_s.at[g])
        for g in range(nz)
    ]
    for load in loads:
        load.start()
    loads[0].wait()

    def score_group(g):
        loads[1 + g].wait()
        at = pair_rows(g)
        s = lax.dot_general(
            cent[...], emb[at, :], (((1,), (1,)), ((), ())), preferred_element_type=f32
        ) * sharp[:, at]
        top = jnp.max(s, axis=0, keepdims=True)
        w = jnp.exp(s - top)
        weights[:, at] = w
        stats[g, j, 0:1, :] = top
        stats[g, j, 1:2, :] = jnp.sum(w, axis=0, keepdims=True)

    def send_stats(g):
        here = stats.at[g, j]
        for d in range(1, n_cent):
            go(remote(
                here, here, st_s.at[g, d - 1], st_r.at[g, d - 1],
                {"cent": lax.rem(j + d, n_cent)},
            ))

    def respond(g):
        for d in range(1, n_cent):
            there = stats.at[g, lax.rem(j + n_cent - d, n_cent)]
            remote(there, there, st_s.at[g, d - 1], st_r.at[g, d - 1], partner).wait_recv()
        tops = [stats[g, c, 0:1, :] for c in range(n_cent)]
        top = functools.reduce(jnp.maximum, tops)
        total = functools.reduce(
            jnp.add, [stats[g, c, 1:2, :] * jnp.exp(tops[c] - top) for c in range(n_cent)]
        )
        scale = jnp.exp(stats[g, j, 0:1, :] - top) / total
        r = weights[:, pair_rows(g)] * scale
        resp_t[:, pair_rows(g)] = r.astype(bf16)
        for h in range(2):
            resp[h, rows_at(g), :] = r[:, h * share:(h + 1) * share].T.astype(bf16)

    def columns(s):
        owner = lax.rem(i + 1 + s, n_dp)
        return pl.ds(pl.multiple_of(owner * width, LANES), width)

    def y_copy(s, zz):
        at = rows_at(zz)
        return remote(y_out.at[s, at], y_in.at[s, at], y_s.at[s, zz], y_r.at[s, zz], partner)

    def mix_group(s, g):
        at = rows_at(g)
        y_out[s, at, :] = jnp.dot(
            resp[1 - y, at, :], cent[:, columns(s)], preferred_element_type=f32
        ).astype(bf16)
        go(y_copy(s, g))

    def mix_other(s):
        y_out[s] = jnp.dot(
            resp[1 - y], cent[:, columns(s)], preferred_element_type=f32
        ).astype(bf16)
        for d in order + [0]:
            go(y_copy(s, lax.rem(z + d, nz)))

    def mix_own(s):
        y_own[s] = jnp.dot(resp[y], cent[:, columns(s)], preferred_element_type=f32)

    def z_reduce(s):
        for d in order:
            tz = lax.rem(z + d, nz)
            at = rows_at(tz)
            y_copy(s, tz).wait_recv()
            value = y_own[s, at, :] + y_in[s, at, :].astype(f32)
            direct = remote(
                z_out.at[s, at], z_in.at[s, d - 1], z_s.at[s, d - 1], z_r.at[s, d - 1], zdev(tz)
            )
            z_out[s, at, :] = value.astype(bf16)
            if not relay:
                go(direct)
            elif d == 2:
                @pl.when(inner)
                def _():
                    remote(
                        z_rel.at[s], z_rel.at[s], rl_s.at[s], rl_r.at[s], partner
                    ).wait_recv()
                    z_out[s, at, :] = (value + z_rel[s].astype(f32)).astype(bf16)

                go(direct)
            else:
                far = at_last if d == 1 else at_first
                via = z - 1 if d == 1 else z + 1
                go_if(jnp.logical_not(far), direct)
                go_if(far, remote(
                    z_out.at[s, at], z_rel.at[s], rl_s.at[s], rl_r.at[s],
                    zdev(jnp.clip(via, 0, nz - 1)),
                ))

    def residual(s):
        at = rows_at(z)
        y_copy(s, z).wait_recv()
        z_acc[...] = y_own[s, at, :] + y_in[s, at, :].astype(f32)
        for d in order:
            def take(d=d):
                there = z_in.at[s, d - 1]
                remote(there, there, z_s.at[s, d - 1], z_r.at[s, d - 1], partner).wait_recv()
                z_acc[...] += z_in[s, d - 1].astype(f32)

            if relay and d != 2:
                pl.when(jnp.logical_not(at_first if d == 1 else at_last))(take)
            else:
                take()
        value = (emb[rows_at(j), columns(s)].astype(f32) - z_acc[...]).astype(bf16)
        out_res[:, columns(s)] = value
        res[s, place(z, y), :] = value
        here = res.at[s, place(z, y)]
        spread(here, lambda d: (gz_s.at[s, d - 1], gz_r.at[s, d - 1]))
        go(remote(here, here, gy_s.at[s, 0], gy_r.at[s, 0], partner))

    z_order = [2, 1, 3] if relay else order

    def spread(here, sems):
        for d in z_order:
            copy = remote(here, here, *sems(d), zdev(lax.rem(z + d, nz)))
            if relay and d != 2:
                go_if(jnp.logical_not(at_last if d == 1 else at_first), copy)
            else:
                go(copy)

    def forward(s):
        for d in z_order:
            here = res.at[s, place(lax.rem(z + nz - d, nz), y)]
            remote(here, here, gz_s.at[s, d - 1], gz_r.at[s, d - 1], partner).wait_recv()
            if relay and d == 2:
                go_if(z == 2, remote(here, here, gf_s.at[s], gz_r.at[s, 2], zdev(3)))
                go_if(z == 1, remote(here, here, gf_x.at[s], gz_r.at[s, 0], zdev(0)))
            go(remote(here, here, gy_s.at[s, d], gy_r.at[s, d], partner))

    kb = min(k, 512)

    def update(s):
        for d in range(nz):
            there = res.at[s, place(lax.rem(z + nz - d, nz), 1 - y)]
            remote(there, there, gy_s.at[s, d], gy_r.at[s, d], partner).wait_recv()

        def step(b, _):
            at = pl.ds(pl.multiple_of(b * kb, kb), kb)
            u = jnp.dot(resp_t[at, :], res[s], preferred_element_type=f32)
            if s < n_dp - 1:
                upd_out[s, at, :] = u.astype(bf16)
            else:
                upd_own[at, :] = u
            return 0

        lax.fori_loop(0, k // kb, step, 0)
        if s < n_dp - 1:
            go(remote(
                upd_out.at[s], upd_in.at[s], u_s.at[s], u_r.at[s],
                {"dp": lax.rem(i + 1 + s, n_dp)},
            ))

    def share_rows_dp(buf, s_sem, r_sem):
        for d in range(1, n_dp):
            go(remote(
                buf.at[0], buf.at[d], s_sem.at[d - 1], r_sem.at[d - 1],
                {"dp": lax.rem(i + d, n_dp)},
            ))

    def sum_rows_dp(buf, s_sem, r_sem):
        acc = buf[0]
        for d in range(1, n_dp):
            remote(
                buf.at[0], buf.at[d], s_sem.at[d - 1], r_sem.at[d - 1],
                {"dp": lax.rem(i + d, n_dp)},
            ).wait_recv()
            acc += buf[d]
        return jnp.broadcast_to(acc[0:1], (LANES, k)).T[:, 0:1]

    score_group(0)
    pl.semaphore_wait(barrier, n_cent - 1 + n_dp - 1)
    send_stats(0)
    lead = min(3, nz)
    for g in range(1, lead):
        score_group(g)
        send_stats(g)
    for g in range(nz):
        respond(g)
        mix_group(0, g)
        if g + lead < nz:
            score_group(g + lead)
            send_stats(g + lead)
    mix_own(0)
    mix_other(1)
    mix_own(1)
    cnt[0] = lax.dot_general(
        jnp.ones((8, rows), bf16), resp_t[...], (((1,), (1,)), ((), ())),
        preferred_element_type=f32,
    )
    share_rows_dp(cnt, c_s, c_r)

    for t in range(n_dp + 3):
        if t < n_dp:
            z_reduce(t)
        if t + 2 < n_dp:
            mix_other(t + 2)
            mix_own(t + 2)
        if 0 <= t - 1 < n_dp:
            residual(t - 1)
        if 0 <= t - 2 < n_dp:
            forward(t - 2)
        if 0 <= t - 3 < n_dp:
            update(t - 3)

    inv = 1.0 / (sum_rows_dp(cnt, c_s, c_r) + 1.0)
    acc = upd_own[...]
    for s in range(n_dp - 1):
        remote(
            upd_out.at[s], upd_in.at[s], u_s.at[s], u_r.at[s], {"dp": lax.rem(i + 1 + s, n_dp)}
        ).wait_recv()
        acc += upd_in[s].astype(f32)
    own = pl.ds(pl.multiple_of(i * width, LANES), width)
    moved = cent[:, own].astype(f32) + acc * inv
    upd_own[...] = moved
    squares = jnp.sum(moved * moved, axis=1, keepdims=True)
    sq[0] = jnp.broadcast_to(squares, (k, LANES)).T[0:8]
    share_rows_dp(sq, q_s, q_r)
    norm = lax.rsqrt(sum_rows_dp(sq, q_s, q_r) + 1e-06)
    out_cent[...] = upd_own[...] * norm
    for wait in pending:
        wait()


def hand_over(a, b, out_a, out_b):
    out_a[...] = a[...]
    out_b[...] = b[...]


def per_device_fused(n_dp, n_cent, embeddings, sharpness, centroids):
    f32, bf16 = jnp.float32, jnp.bfloat16
    rows, depth = embeddings.shape
    k = centroids.shape[0]
    width = depth // n_dp
    nz = n_cent // 2
    share = rows // n_cent
    half = nz * share
    vmem = pl.BlockSpec(memory_space=pltpu.VMEM)
    hbm = pl.BlockSpec(memory_space=pl.ANY)
    dma = lambda *shape: pltpu.SemaphoreType.DMA(shape)
    pairs = lambda *shape: [dma(*shape), dma(*shape)]
    moved, own = pl.pallas_call(
        functools.partial(kernel, n_dp, n_cent),
        out_shape=(
            jax.ShapeDtypeStruct((k, width), f32),
            jax.ShapeDtypeStruct((share, depth), bf16),
        ),
        in_specs=[hbm, vmem, hbm],
        out_specs=(vmem, vmem),
        scratch_shapes=[
            pltpu.VMEM((rows, depth), bf16),
            pltpu.VMEM((k, depth), bf16),
            pltpu.VMEM((k, rows), f32),
            pltpu.VMEM((k, rows), bf16),
            pltpu.VMEM((2, half, k), bf16),
            pltpu.VMEM((nz, n_cent, 2, 2 * share), f32),
            pltpu.VMEM((n_dp, half, width), bf16),
            pltpu.VMEM((n_dp, half, width), bf16),
            pltpu.VMEM((n_dp, half, width), f32),
            pltpu.VMEM((n_dp, half, width), bf16),
            pltpu.VMEM((n_dp, nz - 1, share, width), bf16),
            pltpu.VMEM((n_dp, share, width), bf16),
            pltpu.VMEM((share, width), f32),
            pltpu.VMEM((n_dp, rows, width), bf16),
            pltpu.VMEM((n_dp - 1, k, width), bf16),
            pltpu.VMEM((n_dp - 1, k, width), bf16),
            pltpu.VMEM((k, width), f32),
            pltpu.VMEM((n_dp, 8, k), f32),
            pltpu.VMEM((n_dp, 8, k), f32),
        ]
        + pairs(nz, n_cent - 1)
        + pairs(n_dp, nz)
        + pairs(n_dp, nz - 1)
        + pairs(n_dp)
        + pairs(n_dp, nz - 1)
        + pairs(n_dp)
        + pairs(n_dp, nz)
        + pairs(n_dp - 1)
        + pairs(n_dp - 1)
        + pairs(n_dp - 1)
        + [dma(nz + 1)],
        compiler_params=pltpu.CompilerParams(
            collective_id=0, has_side_effects=True, vmem_limit_bytes=56 * 2**20
        ),
    )(embeddings, sharpness.reshape(1, rows), centroids)
    steps = 4
    blocks = [
        pl.BlockSpec((k // steps, width), lambda t: (t, 0)),
        pl.BlockSpec((share // steps, depth), lambda t: (t, 0)),
    ]
    return pl.pallas_call(
        hand_over,
        grid=(steps,),
        out_shape=(
            jax.ShapeDtypeStruct((k, width), f32),
            jax.ShapeDtypeStruct((share, depth), bf16),
        ),
        in_specs=blocks,
        out_specs=tuple(blocks),
    )(moved, own)


def solution(mesh):
    n_dp, n_cent = mesh.shape["dp"], mesh.shape["cent"]

    def per_device(embeddings, sharpness, centroids):
        rows, depth = embeddings.shape
        fits = (
            n_dp > 1
            and n_cent % 4 == 0
            and depth % (n_dp * LANES) == 0
            and rows % (n_cent * LANES) == 0
            and centroids.shape[0] % 512 == 0
        )
        if fits:
            return per_device_fused(n_dp, n_cent, embeddings, sharpness, centroids)
        return per_device_plain(embeddings, sharpness, centroids)

    in_specs = (P("dp", None), P("dp"), P("cent", None))
    out_specs = (P("cent", "dp"), P(("dp", "cent"), None))
    return jax.shard_map(
        per_device, mesh=mesh, in_specs=in_specs, out_specs=out_specs, check_vma=False
    )
```

```python
import functools

import jax
import jax.numpy as jnp
from jax import lax
from jax.experimental import pallas as pl
from jax.experimental.pallas import tpu as pltpu
from jax.sharding import PartitionSpec as P

MESH = pl.DeviceIdType.MESH
LANES = 128


def per_device_plain(embeddings, sharpness, centroids):
    scores = lax.dot_general(
        embeddings, centroids, (((1,), (1,)), ((), ())), preferred_element_type=jnp.float32
    )
    scores = scores * sharpness[:, None]
    row_top = lax.pmax(jnp.max(scores, axis=1), "cent")
    weights = jnp.exp(scores - row_top[:, None])
    row_total = lax.psum(jnp.sum(weights, axis=1), "cent")
    responsibility = (weights / row_total[:, None]).astype(jnp.bfloat16)
    partial_mixture = jnp.dot(responsibility, centroids, preferred_element_type=jnp.float32)
    share_rows = embeddings.shape[0] // lax.axis_size("cent")
    row_start = lax.axis_index("cent") * share_rows
    mixture_share = lax.psum_scatter(partial_mixture, "cent", scatter_dimension=0, tiled=True)
    own_rows = lax.dynamic_slice_in_dim(embeddings, row_start, share_rows, 0)
    own_residual = (own_rows.astype(jnp.float32) - mixture_share).astype(jnp.bfloat16)
    all_residual = lax.all_gather(own_residual, "cent", axis=0, tiled=True)
    count_part = jnp.sum(responsibility.astype(jnp.float32), axis=0)
    update = lax.dot_general(
        responsibility, all_residual, (((0,), (0,)), ((), ())), preferred_element_type=jnp.float32
    )
    width = centroids.shape[1] // lax.axis_size("dp")
    column_start = lax.axis_index("dp") * width
    centroid_cols = lax.dynamic_slice_in_dim(centroids, column_start, width, 1).astype(jnp.float32)
    counts = lax.psum(count_part, "dp")
    update_share = lax.psum_scatter(
        update.astype(jnp.bfloat16), "dp", scatter_dimension=1, tiled=True
    ).astype(jnp.float32)
    moved = centroid_cols + update_share / (counts[:, None] + 1.0)
    squares = lax.psum(jnp.sum(moved * moved, axis=1), "dp")
    new_centroids = moved * lax.rsqrt(squares + 1e-06)[:, None]
    return (new_centroids, own_residual)


def remote(src, dst, send_sem, recv_sem, target):
    return pltpu.make_async_remote_copy(
        src_ref=src, dst_ref=dst, send_sem=send_sem, recv_sem=recv_sem,
        device_id=target, device_id_type=MESH,
    )


def kernel(
    n_dp, n_cent, emb, sharp, cent, out_cent, out_res,
    weights, resp_t, resp, scales, stats, y_out, y_in, y_own, z_out, z_in, z_rel, z_acc, res,
    upd_out, upd_in, upd_own, cnt, sq,
    st_s, st_r, y_s, y_r, z_s, z_r, rl_s, rl_r, gz_s, gz_r, gf_s, gf_x, gy_s, gy_r,
    u_s, u_r, c_s, c_r, q_s, q_r,
):
    f32, bf16 = jnp.float32, jnp.bfloat16
    rows, depth = emb.shape
    k = cent.shape[0]
    width = depth // n_dp
    nz = n_cent // 2
    share = rows // n_cent
    half = nz * share
    groups = nz // 2
    pair = 2 * share
    relay = nz == 4
    i = lax.axis_index("dp")
    j = lax.axis_index("cent")
    z, y = j // 2, j % 2
    partner = {"cent": z * 2 + (1 - y)}
    inner = jnp.logical_and(z > 0, z < nz - 1)
    at_first, at_last = z == 0, z == nz - 1
    order = [nz - 1] + list(range(1, nz - 1)) if nz > 2 else [1]

    def rows_at(index):
        return pl.ds(pl.multiple_of(index * share, share), share)

    def place(zz, yy):
        return rows_at(yy * nz + zz)

    def zdev(zz):
        return {"cent": zz * 2 + y}

    barrier = pltpu.get_barrier_semaphore()
    for d in range(1, n_cent):
        pl.semaphore_signal(
            barrier, inc=1, device_id={"cent": lax.rem(j + d, n_cent)}, device_id_type=MESH
        )
    for d in range(1, n_dp):
        pl.semaphore_signal(
            barrier, inc=1, device_id={"dp": lax.rem(i + d, n_dp)}, device_id_type=MESH
        )

    pending = []

    def go(copy):
        copy.start()
        pending.append(copy.wait_send)

    def go_if(cond, copy):
        pl.when(cond)(copy.start)
        pending.append(lambda: pl.when(cond)(copy.wait_send))

    def score_group(g):
        def half_block(h, _):
            e = jnp.concatenate([emb[rows_at(4 * g + h), :], emb[rows_at(4 * g + 2 + h), :]], 0)
            sh = jnp.concatenate(
                [sharp[:, rows_at(4 * g + h)], sharp[:, rows_at(4 * g + 2 + h)]], 1
            )
            s = lax.dot_general(
                cent[...], e, (((1,), (1,)), ((), ())), preferred_element_type=f32
            ) * sh
            top = jnp.max(s, axis=0, keepdims=True)
            w = jnp.exp(s - top)
            weights[:, pl.ds(pl.multiple_of(h * half + g * pair, share), pair)] = w
            at = pl.ds(pl.multiple_of(h * pair, share), pair)
            resp[h, pl.ds(g * pair, pair), :] = w.T.astype(bf16)
            stats[g, j, 0:1, at] = top
            stats[g, j, 1:2, at] = jnp.sum(w, axis=0, keepdims=True)
            return 0

        lax.fori_loop(0, 2, half_block, 0)

    def send_stats(g):
        here = stats.at[g, j]
        for d in range(1, n_cent):
            go(remote(
                here, here, st_s.at[g, d - 1], st_r.at[g, d - 1],
                {"cent": lax.rem(j + d, n_cent)},
            ))

    def respond(g):
        for d in range(1, n_cent):
            there = stats.at[g, lax.rem(j + n_cent - d, n_cent)]
            remote(there, there, st_s.at[g, d - 1], st_r.at[g, d - 1], partner).wait_recv()
        tops = [stats[g, c, 0:1, :] for c in range(n_cent)]
        top = functools.reduce(jnp.maximum, tops)
        total = functools.reduce(
            jnp.add, [stats[g, c, 1:2, :] * jnp.exp(tops[c] - top) for c in range(n_cent)]
        )
        stats[g, n_cent, 0:1, :] = jnp.exp(stats[g, j, 0:1, :] - top) / total
        stats[g, n_cent, 1:2, :] = jnp.exp(stats[g, z * 2 + 1 - y, 0:1, :] - top) / total
        mine = pl.ds(pl.multiple_of(y * pair, share), pair)
        for who in range(2):
            scales[who, pl.ds(g * pair, pair), :] = jnp.broadcast_to(
                stats[g, n_cent, who:who + 1, mine], (LANES, pair)
            ).T

        def block(b, _):
            h, q = b // 2, b % 2
            at = place(2 * g + q, h)
            r = weights[:, at] * stats[g, n_cent, 0:1, rows_at(b)]
            resp_t[:, at] = r.astype(bf16)
            return 0

        lax.fori_loop(0, 4, block, 0)

    def columns(s):
        owner = lax.rem(i + 1 + s, n_dp)
        return pl.ds(pl.multiple_of(owner * width, LANES), width)

    def y_copy(s, zz):
        at = rows_at(zz)
        return remote(y_out.at[s, at], y_in.at[s, at], y_s.at[s, zz], y_r.at[s, zz], partner)

    def mix_group(s, g):
        at = pl.ds(g * pair, pair)
        y_out[s, at, :] = jnp.dot(
            resp[1 - y, at, :], cent[:, columns(s)], preferred_element_type=f32
        ).astype(bf16)
        for q in range(2):
            go(y_copy(s, 2 * g + q))

    def mix_other(s):
        y_out[s] = jnp.dot(
            resp[1 - y], cent[:, columns(s)], preferred_element_type=f32
        ).astype(bf16)
        for d in order + [0]:
            go(y_copy(s, lax.rem(z + d, nz)))

    def mix_own(s):
        y_own[s] = jnp.dot(resp[y], cent[:, columns(s)], preferred_element_type=f32)

    def y_sum(s, at):
        return (
            y_own[s, at, :] * scales[0, at, 0:1]
            + y_in[s, at, :].astype(f32) * scales[1, at, 0:1]
        )

    def z_reduce(s):
        for d in order:
            tz = lax.rem(z + d, nz)
            at = rows_at(tz)
            y_copy(s, tz).wait_recv()
            value = y_sum(s, at)
            direct = remote(
                z_out.at[s, at], z_in.at[s, d - 1], z_s.at[s, d - 1], z_r.at[s, d - 1], zdev(tz)
            )
            z_out[s, at, :] = value.astype(bf16)
            if not relay:
                go(direct)
            elif d == 2:
                @pl.when(inner)
                def _():
                    remote(
                        z_rel.at[s], z_rel.at[s], rl_s.at[s], rl_r.at[s], partner
                    ).wait_recv()
                    z_out[s, at, :] = (value + z_rel[s].astype(f32)).astype(bf16)

                go(direct)
            else:
                far = at_last if d == 1 else at_first
                via = z - 1 if d == 1 else z + 1
                go_if(jnp.logical_not(far), direct)
                go_if(far, remote(
                    z_out.at[s, at], z_rel.at[s], rl_s.at[s], rl_r.at[s],
                    zdev(jnp.clip(via, 0, nz - 1)),
                ))

    def residual(s):
        at = rows_at(z)
        y_copy(s, z).wait_recv()
        z_acc[...] = y_sum(s, at)
        for d in order:
            def take(d=d):
                there = z_in.at[s, d - 1]
                remote(there, there, z_s.at[s, d - 1], z_r.at[s, d - 1], partner).wait_recv()
                z_acc[...] += z_in[s, d - 1].astype(f32)

            if relay and d != 2:
                pl.when(jnp.logical_not(at_first if d == 1 else at_last))(take)
            else:
                take()
        value = (emb[rows_at(j), columns(s)].astype(f32) - z_acc[...]).astype(bf16)
        out_res[:, columns(s)] = value
        res[s, place(z, y), :] = value
        here = res.at[s, place(z, y)]
        for d in ([2, 1, 3] if relay else order):
            copy = remote(
                here, here, gz_s.at[s, d - 1], gz_r.at[s, d - 1], zdev(lax.rem(z + d, nz))
            )
            if relay and d != 2:
                go_if(jnp.logical_not(at_last if d == 1 else at_first), copy)
            else:
                go(copy)
        go(remote(here, here, gy_s.at[s, 0], gy_r.at[s, 0], partner))

    def forward(s):
        for d in ([2, 1, 3] if relay else order):
            here = res.at[s, place(lax.rem(z + nz - d, nz), y)]
            remote(here, here, gz_s.at[s, d - 1], gz_r.at[s, d - 1], partner).wait_recv()
            if relay and d == 2:
                go_if(z == 2, remote(here, here, gf_s.at[s], gz_r.at[s, 2], zdev(3)))
                go_if(z == 1, remote(here, here, gf_x.at[s], gz_r.at[s, 0], zdev(0)))
            go(remote(here, here, gy_s.at[s, d], gy_r.at[s, d], partner))

    kb = min(k, 512)

    def update(s):
        for d in range(nz):
            there = res.at[s, place(lax.rem(z + nz - d, nz), 1 - y)]
            remote(there, there, gy_s.at[s, d], gy_r.at[s, d], partner).wait_recv()

        def step(b, _):
            at = pl.ds(pl.multiple_of(b * kb, kb), kb)
            u = jnp.dot(resp_t[at, :], res[s], preferred_element_type=f32)
            if s < n_dp - 1:
                upd_out[s, at, :] = u.astype(bf16)
            else:
                upd_own[at, :] = u
            return 0

        lax.fori_loop(0, k // kb, step, 0)
        if s < n_dp - 1:
            go(remote(
                upd_out.at[s], upd_in.at[s], u_s.at[s], u_r.at[s],
                {"dp": lax.rem(i + 1 + s, n_dp)},
            ))

    def share_rows_dp(buf, s_sem, r_sem):
        for d in range(1, n_dp):
            go(remote(
                buf.at[0], buf.at[d], s_sem.at[d - 1], r_sem.at[d - 1],
                {"dp": lax.rem(i + d, n_dp)},
            ))

    def sum_rows_dp(buf, s_sem, r_sem):
        acc = buf[0]
        for d in range(1, n_dp):
            remote(
                buf.at[0], buf.at[d], s_sem.at[d - 1], r_sem.at[d - 1],
                {"dp": lax.rem(i + d, n_dp)},
            ).wait_recv()
            acc += buf[d]
        return jnp.broadcast_to(acc[0:1], (LANES, k)).T[:, 0:1]

    score_group(0)
    pl.semaphore_wait(barrier, n_cent - 1 + n_dp - 1)
    send_stats(0)
    mix_group(0, 0)
    for g in range(1, groups):
        score_group(g)
        send_stats(g)
        mix_group(0, g)
    mix_own(0)
    mix_other(1)
    mix_own(1)
    for g in range(groups):
        respond(g)
    cnt[0] = lax.dot_general(
        jnp.ones((8, rows), bf16), resp_t[...], (((1,), (1,)), ((), ())),
        preferred_element_type=f32,
    )
    share_rows_dp(cnt, c_s, c_r)

    for t in range(n_dp + 3):
        if t < n_dp:
            z_reduce(t)
        if t + 2 < n_dp:
            mix_other(t + 2)
            mix_own(t + 2)
        if 0 <= t - 1 < n_dp:
            residual(t - 1)
        if 0 <= t - 2 < n_dp:
            forward(t - 2)
        if 0 <= t - 3 < n_dp:
            update(t - 3)

    inv = 1.0 / (sum_rows_dp(cnt, c_s, c_r) + 1.0)
    acc = upd_own[...]
    for s in range(n_dp - 1):
        remote(
            upd_out.at[s], upd_in.at[s], u_s.at[s], u_r.at[s], {"dp": lax.rem(i + 1 + s, n_dp)}
        ).wait_recv()
        acc += upd_in[s].astype(f32)
    own = pl.ds(pl.multiple_of(i * width, LANES), width)
    moved = cent[:, own].astype(f32) + acc * inv
    upd_own[...] = moved
    squares = jnp.sum(moved * moved, axis=1, keepdims=True)
    sq[0] = jnp.broadcast_to(squares, (k, LANES)).T[0:8]
    share_rows_dp(sq, q_s, q_r)
    norm = lax.rsqrt(sum_rows_dp(sq, q_s, q_r) + 1e-06)
    out_cent[...] = upd_own[...] * norm
    for wait in pending:
        wait()


def per_device_fused(n_dp, n_cent, embeddings, sharpness, centroids):
    f32, bf16 = jnp.float32, jnp.bfloat16
    rows, depth = embeddings.shape
    k = centroids.shape[0]
    width = depth // n_dp
    nz = n_cent // 2
    share = rows // n_cent
    half = nz * share
    vmem = pl.BlockSpec(memory_space=pltpu.VMEM)
    dma = lambda *shape: pltpu.SemaphoreType.DMA(shape)
    pairs = lambda *shape: [dma(*shape), dma(*shape)]
    return pl.pallas_call(
        functools.partial(kernel, n_dp, n_cent),
        out_shape=(
            jax.ShapeDtypeStruct((k, width), f32),
            jax.ShapeDtypeStruct((share, depth), bf16),
        ),
        in_specs=[vmem] * 3,
        out_specs=(vmem, vmem),
        scratch_shapes=[
            pltpu.VMEM((k, rows), f32),
            pltpu.VMEM((k, rows), bf16),
            pltpu.VMEM((2, half, k), bf16),
            pltpu.VMEM((2, half, LANES), f32),
            pltpu.VMEM((nz // 2, n_cent + 1, 2, 4 * share), f32),
            pltpu.VMEM((n_dp, half, width), bf16),
            pltpu.VMEM((n_dp, half, width), bf16),
            pltpu.VMEM((n_dp, half, width), f32),
            pltpu.VMEM((n_dp, half, width), bf16),
            pltpu.VMEM((n_dp, nz - 1, share, width), bf16),
            pltpu.VMEM((n_dp, share, width), bf16),
            pltpu.VMEM((share, width), f32),
            pltpu.VMEM((n_dp, rows, width), bf16),
            pltpu.VMEM((n_dp - 1, k, width), bf16),
            pltpu.VMEM((n_dp - 1, k, width), bf16),
            pltpu.VMEM((k, width), f32),
            pltpu.VMEM((n_dp, 8, k), f32),
            pltpu.VMEM((n_dp, 8, k), f32),
        ]
        + pairs(nz // 2, n_cent - 1)
        + pairs(n_dp, nz)
        + pairs(n_dp, nz - 1)
        + pairs(n_dp)
        + pairs(n_dp, nz - 1)
        + pairs(n_dp)
        + pairs(n_dp, nz)
        + pairs(n_dp - 1)
        + pairs(n_dp - 1)
        + pairs(n_dp - 1),
        compiler_params=pltpu.CompilerParams(
            collective_id=0, has_side_effects=True, vmem_limit_bytes=56 * 2**20
        ),
    )(embeddings, sharpness.reshape(1, rows), centroids)


def solution(mesh):
    n_dp, n_cent = mesh.shape["dp"], mesh.shape["cent"]

    def per_device(embeddings, sharpness, centroids):
        rows, depth = embeddings.shape
        fits = (
            n_dp > 1
            and n_cent % 4 == 0
            and depth % (n_dp * LANES) == 0
            and rows % (n_cent * LANES) == 0
            and centroids.shape[0] % 512 == 0
        )
        if fits:
            return per_device_fused(n_dp, n_cent, embeddings, sharpness, centroids)
        return per_device_plain(embeddings, sharpness, centroids)

    in_specs = (P("dp", None), P("dp"), P("cent", None))
    out_specs = (P("cent", "dp"), P(("dp", "cent"), None))
    return jax.shard_map(
        per_device, mesh=mesh, in_specs=in_specs, out_specs=out_specs, check_vma=False
    )
```

```python
import functools

import jax
import jax.numpy as jnp
from jax import lax
from jax.experimental import pallas as pl
from jax.experimental.pallas import tpu as pltpu
from jax.sharding import PartitionSpec as P

MESH = pl.DeviceIdType.MESH
LANES = 128


def per_device_plain(embeddings, sharpness, centroids):
    scores = lax.dot_general(
        embeddings, centroids, (((1,), (1,)), ((), ())), preferred_element_type=jnp.float32
    )
    scores = scores * sharpness[:, None]
    row_top = lax.pmax(jnp.max(scores, axis=1), "cent")
    weights = jnp.exp(scores - row_top[:, None])
    row_total = lax.psum(jnp.sum(weights, axis=1), "cent")
    responsibility = (weights / row_total[:, None]).astype(jnp.bfloat16)
    partial_mixture = jnp.dot(responsibility, centroids, preferred_element_type=jnp.float32)
    share_rows = embeddings.shape[0] // lax.axis_size("cent")
    row_start = lax.axis_index("cent") * share_rows
    mixture_share = lax.psum_scatter(partial_mixture, "cent", scatter_dimension=0, tiled=True)
    own_rows = lax.dynamic_slice_in_dim(embeddings, row_start, share_rows, 0)
    own_residual = (own_rows.astype(jnp.float32) - mixture_share).astype(jnp.bfloat16)
    all_residual = lax.all_gather(own_residual, "cent", axis=0, tiled=True)
    count_part = jnp.sum(responsibility.astype(jnp.float32), axis=0)
    update = lax.dot_general(
        responsibility, all_residual, (((0,), (0,)), ((), ())), preferred_element_type=jnp.float32
    )
    width = centroids.shape[1] // lax.axis_size("dp")
    column_start = lax.axis_index("dp") * width
    centroid_cols = lax.dynamic_slice_in_dim(centroids, column_start, width, 1).astype(jnp.float32)
    counts = lax.psum(count_part, "dp")
    update_share = lax.psum_scatter(
        update.astype(jnp.bfloat16), "dp", scatter_dimension=1, tiled=True
    ).astype(jnp.float32)
    moved = centroid_cols + update_share / (counts[:, None] + 1.0)
    squares = lax.psum(jnp.sum(moved * moved, axis=1), "dp")
    new_centroids = moved * lax.rsqrt(squares + 1e-06)[:, None]
    return (new_centroids, own_residual)


def remote(src, dst, send_sem, recv_sem, target):
    return pltpu.make_async_remote_copy(
        src_ref=src, dst_ref=dst, send_sem=send_sem, recv_sem=recv_sem,
        device_id=target, device_id_type=MESH,
    )


def kernel(
    n_dp, n_cent, emb, sharp, cent, out_cent, out_res,
    weights, resp_t, resp, stats, y_out, y_in, y_own, z_out, z_in, z_rel, z_acc, res,
    upd_out, upd_in, upd_own, cnt, sq,
    st_s, st_r, y_s, y_r, z_s, z_r, rl_s, rl_r, gz_s, gz_r, gf_s, gf_x, gy_s, gy_r,
    u_s, u_r, c_s, c_r, q_s, q_r,
):
    f32, bf16 = jnp.float32, jnp.bfloat16
    rows, depth = emb.shape
    k = cent.shape[0]
    width = depth // n_dp
    nz = n_cent // 2
    share = rows // n_cent
    half = nz * share
    groups = nz // 2
    pair = 2 * share
    relay = nz == 4
    i = lax.axis_index("dp")
    j = lax.axis_index("cent")
    z, y = j // 2, j % 2
    partner = {"cent": z * 2 + (1 - y)}
    ix, ic = i // 2, i % 2
    sibling = ix * 2 + (1 - ic)
    owners = [(1 - ix) * 2 + (1 - ic), (1 - ix) * 2 + ic, sibling, i]
    targets = [sibling, owners[1], sibling]
    inner = jnp.logical_and(z > 0, z < nz - 1)
    at_first, at_last = z == 0, z == nz - 1
    order = [nz - 1] + list(range(1, nz - 1)) if nz > 2 else [1]

    def rows_at(index):
        return pl.ds(pl.multiple_of(index * share, share), share)

    def place(zz, yy):
        return rows_at(yy * nz + zz)

    def zdev(zz):
        return {"cent": zz * 2 + y}

    barrier = pltpu.get_barrier_semaphore()
    for d in range(1, n_cent):
        pl.semaphore_signal(
            barrier, inc=1, device_id={"cent": lax.rem(j + d, n_cent)}, device_id_type=MESH
        )
    for d in range(1, n_dp):
        pl.semaphore_signal(
            barrier, inc=1, device_id={"dp": lax.rem(i + d, n_dp)}, device_id_type=MESH
        )

    pending = []

    def go(copy):
        copy.start()
        pending.append(copy.wait_send)

    def go_if(cond, copy):
        pl.when(cond)(copy.start)
        pending.append(lambda: pl.when(cond)(copy.wait_send))

    def score_group(g):
        def half_block(h, _):
            e = jnp.concatenate([emb[rows_at(4 * g + h), :], emb[rows_at(4 * g + 2 + h), :]], 0)
            sh = jnp.concatenate(
                [sharp[:, rows_at(4 * g + h)], sharp[:, rows_at(4 * g + 2 + h)]], 1
            )
            s = lax.dot_general(
                cent[...], e, (((1,), (1,)), ((), ())), preferred_element_type=f32
            ) * sh
            top = jnp.max(s, axis=0, keepdims=True)
            w = jnp.exp(s - top)
            weights[:, pl.ds(pl.multiple_of(h * half + g * pair, share), pair)] = w
            at = pl.ds(pl.multiple_of(h * pair, share), pair)
            stats[g, j, 0:1, at] = top
            stats[g, j, 1:2, at] = jnp.sum(w, axis=0, keepdims=True)
            return 0

        lax.fori_loop(0, 2, half_block, 0)

    def send_stats(g):
        here = stats.at[g, j]
        for d in range(1, n_cent):
            go(remote(
                here, here, st_s.at[g, d - 1], st_r.at[g, d - 1],
                {"cent": lax.rem(j + d, n_cent)},
            ))

    def respond(g):
        for d in range(1, n_cent):
            there = stats.at[g, lax.rem(j + n_cent - d, n_cent)]
            remote(there, there, st_s.at[g, d - 1], st_r.at[g, d - 1], partner).wait_recv()
        tops = [stats[g, c, 0:1, :] for c in range(n_cent)]
        top = functools.reduce(jnp.maximum, tops)
        total = functools.reduce(
            jnp.add, [stats[g, c, 1:2, :] * jnp.exp(tops[c] - top) for c in range(n_cent)]
        )
        stats[g, n_cent, 0:1, :] = jnp.exp(stats[g, j, 0:1, :] - top) / total

        def block(b, _):
            h, q = b // 2, b % 2
            at = place(2 * g + q, h)
            r = weights[:, at] * stats[g, n_cent, 0:1, rows_at(b)]
            resp_t[:, at] = r.astype(bf16)
            resp[h, rows_at(2 * g + q), :] = r.T.astype(bf16)
            return 0

        lax.fori_loop(0, 4, block, 0)

    def columns(s):
        return pl.ds(pl.multiple_of(owners[s] * width, LANES), width)

    def y_copy(s, zz):
        at = rows_at(zz)
        return remote(y_out.at[s, at], y_in.at[s, at], y_s.at[s, zz], y_r.at[s, zz], partner)

    def mix_group(s, g):
        at = pl.ds(g * pair, pair)
        y_out[s, at, :] = jnp.dot(
            resp[1 - y, at, :], cent[:, columns(s)], preferred_element_type=f32
        ).astype(bf16)
        for q in range(2):
            go(y_copy(s, 2 * g + q))

    def mix_other(s):
        y_out[s] = jnp.dot(
            resp[1 - y], cent[:, columns(s)], preferred_element_type=f32
        ).astype(bf16)
        for d in order + [0]:
            go(y_copy(s, lax.rem(z + d, nz)))

    def mix_own(s):
        y_own[s] = jnp.dot(resp[y], cent[:, columns(s)], preferred_element_type=f32)

    def z_reduce(s):
        for d in order:
            tz = lax.rem(z + d, nz)
            at = rows_at(tz)
            y_copy(s, tz).wait_recv()
            value = y_own[s, at, :] + y_in[s, at, :].astype(f32)
            direct = remote(
                z_out.at[s, at], z_in.at[s, d - 1], z_s.at[s, d - 1], z_r.at[s, d - 1], zdev(tz)
            )
            z_out[s, at, :] = value.astype(bf16)
            if not relay:
                go(direct)
            elif d == 2:
                @pl.when(inner)
                def _():
                    remote(
                        z_rel.at[s], z_rel.at[s], rl_s.at[s], rl_r.at[s], partner
                    ).wait_recv()
                    z_out[s, at, :] = (value + z_rel[s].astype(f32)).astype(bf16)

                go(direct)
            else:
                far = at_last if d == 1 else at_first
                via = z - 1 if d == 1 else z + 1
                go_if(jnp.logical_not(far), direct)
                go_if(far, remote(
                    z_out.at[s, at], z_rel.at[s], rl_s.at[s], rl_r.at[s],
                    zdev(jnp.clip(via, 0, nz - 1)),
                ))

    def residual(s):
        at = rows_at(z)
        y_copy(s, z).wait_recv()
        z_acc[...] = y_own[s, at, :] + y_in[s, at, :].astype(f32)
        for d in order:
            def take(d=d):
                there = z_in.at[s, d - 1]
                remote(there, there, z_s.at[s, d - 1], z_r.at[s, d - 1], partner).wait_recv()
                z_acc[...] += z_in[s, d - 1].astype(f32)

            if relay and d != 2:
                pl.when(jnp.logical_not(at_first if d == 1 else at_last))(take)
            else:
                take()
        value = (emb[rows_at(j), columns(s)].astype(f32) - z_acc[...]).astype(bf16)
        out_res[:, columns(s)] = value
        res[s, place(z, y), :] = value
        here = res.at[s, place(z, y)]
        for d in ([2, 1, 3] if relay else order):
            copy = remote(
                here, here, gz_s.at[s, d - 1], gz_r.at[s, d - 1], zdev(lax.rem(z + d, nz))
            )
            if relay and d != 2:
                go_if(jnp.logical_not(at_last if d == 1 else at_first), copy)
            else:
                go(copy)
        go(remote(here, here, gy_s.at[s, 0], gy_r.at[s, 0], partner))

    def forward(s):
        for d in ([2, 1, 3] if relay else order):
            here = res.at[s, place(lax.rem(z + nz - d, nz), y)]
            remote(here, here, gz_s.at[s, d - 1], gz_r.at[s, d - 1], partner).wait_recv()
            if relay and d == 2:
                go_if(z == 2, remote(here, here, gf_s.at[s], gz_r.at[s, 2], zdev(3)))
                go_if(z == 1, remote(here, here, gf_x.at[s], gz_r.at[s, 0], zdev(0)))
            go(remote(here, here, gy_s.at[s, d], gy_r.at[s, d], partner))

    kb = min(k, 512)

    def update(s):
        for d in range(nz):
            there = res.at[s, place(lax.rem(z + nz - d, nz), 1 - y)]
            remote(there, there, gy_s.at[s, d], gy_r.at[s, d], partner).wait_recv()

        if s == 1:
            remote(
                upd_out.at[0], upd_in.at[0], u_s.at[0], u_r.at[0], {"dp": targets[0]}
            ).wait_recv()

        def step(b, _):
            at = pl.ds(pl.multiple_of(b * kb, kb), kb)
            u = jnp.dot(resp_t[at, :], res[s], preferred_element_type=f32)
            if s == 1:
                u = u + upd_in[0, at, :].astype(f32)
            if s < n_dp - 1:
                upd_out[s, at, :] = u.astype(bf16)
            else:
                upd_own[at, :] = u
            return 0

        lax.fori_loop(0, k // kb, step, 0)
        if s < n_dp - 1:
            go(remote(
                upd_out.at[s], upd_in.at[s], u_s.at[s], u_r.at[s], {"dp": targets[s]},
            ))

    def share_rows_dp(buf, s_sem, r_sem):
        for d in range(1, n_dp):
            go(remote(
                buf.at[0], buf.at[d], s_sem.at[d - 1], r_sem.at[d - 1],
                {"dp": lax.rem(i + d, n_dp)},
            ))

    def sum_rows_dp(buf, s_sem, r_sem):
        acc = buf[0]
        for d in range(1, n_dp):
            remote(
                buf.at[0], buf.at[d], s_sem.at[d - 1], r_sem.at[d - 1],
                {"dp": lax.rem(i + d, n_dp)},
            ).wait_recv()
            acc += buf[d]
        return jnp.broadcast_to(acc[0:1], (LANES, k)).T[:, 0:1]

    score_group(0)
    pl.semaphore_wait(barrier, n_cent - 1 + n_dp - 1)
    send_stats(0)
    for g in range(1, groups):
        score_group(g)
        send_stats(g)
    for g in range(groups):
        respond(g)
        mix_group(0, g)
    mix_own(0)
    mix_other(1)
    mix_own(1)
    cnt[0] = lax.dot_general(
        jnp.ones((8, rows), bf16), resp_t[...], (((1,), (1,)), ((), ())),
        preferred_element_type=f32,
    )
    share_rows_dp(cnt, c_s, c_r)

    for t in range(n_dp + 3):
        if t < n_dp:
            z_reduce(t)
        if t + 2 < n_dp:
            mix_other(t + 2)
            mix_own(t + 2)
        if 0 <= t - 1 < n_dp:
            residual(t - 1)
        if 0 <= t - 2 < n_dp:
            forward(t - 2)
        if 0 <= t - 3 < n_dp:
            update(t - 3)

    inv = 1.0 / (sum_rows_dp(cnt, c_s, c_r) + 1.0)
    acc = upd_own[...]
    for s in range(1, n_dp - 1):
        remote(
            upd_out.at[s], upd_in.at[s], u_s.at[s], u_r.at[s], {"dp": targets[s]}
        ).wait_recv()
        acc += upd_in[s].astype(f32)
    own = pl.ds(pl.multiple_of(i * width, LANES), width)
    moved = cent[:, own].astype(f32) + acc * inv
    upd_own[...] = moved
    squares = jnp.sum(moved * moved, axis=1, keepdims=True)
    sq[0] = jnp.broadcast_to(squares, (k, LANES)).T[0:8]
    share_rows_dp(sq, q_s, q_r)
    norm = lax.rsqrt(sum_rows_dp(sq, q_s, q_r) + 1e-06)
    out_cent[...] = upd_own[...] * norm
    for wait in pending:
        wait()


def per_device_fused(n_dp, n_cent, embeddings, sharpness, centroids):
    f32, bf16 = jnp.float32, jnp.bfloat16
    rows, depth = embeddings.shape
    k = centroids.shape[0]
    width = depth // n_dp
    nz = n_cent // 2
    share = rows // n_cent
    half = nz * share
    vmem = pl.BlockSpec(memory_space=pltpu.VMEM)
    dma = lambda *shape: pltpu.SemaphoreType.DMA(shape)
    pairs = lambda *shape: [dma(*shape), dma(*shape)]
    return pl.pallas_call(
        functools.partial(kernel, n_dp, n_cent),
        out_shape=(
            jax.ShapeDtypeStruct((k, width), f32),
            jax.ShapeDtypeStruct((share, depth), bf16),
        ),
        in_specs=[vmem] * 3,
        out_specs=(vmem, vmem),
        scratch_shapes=[
            pltpu.VMEM((k, rows), f32),
            pltpu.VMEM((k, rows), bf16),
            pltpu.VMEM((2, half, k), bf16),
            pltpu.VMEM((nz // 2, n_cent + 1, 2, 4 * share), f32),
            pltpu.VMEM((n_dp, half, width), bf16),
            pltpu.VMEM((n_dp, half, width), bf16),
            pltpu.VMEM((n_dp, half, width), f32),
            pltpu.VMEM((n_dp, half, width), bf16),
            pltpu.VMEM((n_dp, nz - 1, share, width), bf16),
            pltpu.VMEM((n_dp, share, width), bf16),
            pltpu.VMEM((share, width), f32),
            pltpu.VMEM((n_dp, rows, width), bf16),
            pltpu.VMEM((n_dp - 1, k, width), bf16),
            pltpu.VMEM((n_dp - 1, k, width), bf16),
            pltpu.VMEM((k, width), f32),
            pltpu.VMEM((n_dp, 8, k), f32),
            pltpu.VMEM((n_dp, 8, k), f32),
        ]
        + pairs(nz // 2, n_cent - 1)
        + pairs(n_dp, nz)
        + pairs(n_dp, nz - 1)
        + pairs(n_dp)
        + pairs(n_dp, nz - 1)
        + pairs(n_dp)
        + pairs(n_dp, nz)
        + pairs(n_dp - 1)
        + pairs(n_dp - 1)
        + pairs(n_dp - 1),
        compiler_params=pltpu.CompilerParams(
            collective_id=0, has_side_effects=True, vmem_limit_bytes=56 * 2**20
        ),
    )(embeddings, sharpness.reshape(1, rows), centroids)


def solution(mesh):
    n_dp, n_cent = mesh.shape["dp"], mesh.shape["cent"]

    def per_device(embeddings, sharpness, centroids):
        rows, depth = embeddings.shape
        fits = (
            n_dp == 4
            and n_cent % 4 == 0
            and depth % (n_dp * LANES) == 0
            and rows % (n_cent * LANES) == 0
            and centroids.shape[0] % 512 == 0
        )
        if fits:
            return per_device_fused(n_dp, n_cent, embeddings, sharpness, centroids)
        return per_device_plain(embeddings, sharpness, centroids)

    in_specs = (P("dp", None), P("dp"), P("cent", None))
    out_specs = (P("cent", "dp"), P(("dp", "cent"), None))
    return jax.shard_map(
        per_device, mesh=mesh, in_specs=in_specs, out_specs=out_specs, check_vma=False
    )
```
